32 devices in a mesh: dp: 4 (over z), shard: 8 (over y, x, core).
Axes of the slice: x: 2, y: 2, z: 4, core: 2. Of those that a mesh axis runs over, the one named last changes fastest.
Arguments:
- head_terms: bfloat16 [512, 8, 256], P('dp', 'shard'), may hold values from -0.375 to 0.375
- inputs: bfloat16 [512, 2, 4096], P('dp'), may hold values from -6 to 6
- owner_list: int32 [8, 256, 1], P('shard'), may hold values from 0 to 3; in each aligned block of 64 rows (0 to 63, 64 to 127, ..., all dimensions but the last counted through in order) at most 32 rows name the same one
- param_slots: bfloat16 [8, 512, 4096], P('shard', 'dp'), may hold values from -3 to 3
- row_state: float32 [8, 512], P('shard', 'dp'), may hold values from 0.25 to 4
- col_state: float32 [8, 4, 4096], P('shard'), may hold values from 0.25 to 4
Outputs:
- new_params: bfloat16 [8, 512, 4096], P('shard', 'dp')
- new_rows: float32 [8, 512], P('shard', 'dp')
- new_cols: float32 [8, 4, 4096], P('shard')
The draws below stay inside these ranges and needn't reach their ends.
Inputs may be any that keep to these rules, and one draw needn't show every extreme that they name: `owner_list`: each head's 256 rows fall into 4 aligned home blocks of 64 rows; within one home block no owner index is named more than 32 times.
All inputs are finite; a program needn't handle non-finite values.
Results may differ from the reference program's by a relative error of at most 0.0012.
Values sent between devices are 32-bit elements; how exact they have to be, the bound alone decides.
No kernel may reach another device: no remote copies, remote signals or barrier semaphores. Data moves between devices by JAX's collectives and lax.ppermute only.
A program may use at most 64 MiB of HBM per device.

```python
import math
import jax
import jax.numpy as jnp
import numpy as np
from jax import lax

D = 4096
DKV = 64
PROJ = 4
HEADS = 8
ROWS_H = 256
TOKENS = 512
BLOCK = 64
PAIR_MOST = 32
SLOTS = 128
N_DP = 4


def with_spikes(drawn, own_key, source, target, blocks, factor):
    def block_of(position):
        return (jnp.arange(drawn.shape[position]) // (drawn.shape[position] // blocks)).reshape((-1,) + (1,) * (drawn.ndim - 1 - position))

    one_side = jax.random.permutation(own_key, blocks)[block_of(target)]
    second = (block_of(target) + blocks // 2) % blocks
    return jnp.where((block_of(source) == one_side) | (block_of(source) == second), factor * drawn, drawn)


def block_scale(stream_key, dims, shards, smallest, high):
    loudness = 1.0
    for dim, parts in shards:
        draws = jax.random.uniform(jax.random.fold_in(jax.random.fold_in(stream_key, 6), dim), (parts,), jnp.float32, smallest / len(shards), high / len(shards))
        loudness = loudness * jnp.repeat(jnp.exp(draws), dims[dim] // parts).reshape((-1,) + (1,) * (len(dims) - 1 - dim))
    return loudness


def shared_out(stream_key, own, number, rows, count, top, reach, lean):
    order = jax.random.permutation(stream_key, count)
    crowded, usual = portions_of(count, rows * top, reach, lean, True), portions_of(count, rows * top, reach, lean, False)
    places = jnp.arange(count)

    def named(sizes, turn):
        used = int((sizes > 0).sum())
        fixed = max(1, used // 4)
        moved = fixed + (places - fixed + turn * (used - fixed)) % max(1, count - fixed)
        return jnp.zeros((count,), jnp.int32).at[order[jnp.where(places < fixed, places, moved)]].set(jnp.asarray(sizes, jnp.int32))

    sizes = jnp.where(number % 4 == 0, named(crowded, number // 4), named(usual, number - number // 4 - 1))
    mixed = jax.random.permutation(jax.random.fold_in(own, 3), count)
    giver, sink = mixed[0:count // 2 * 2:2], mixed[1:count // 2 * 2:2]
    margin = jnp.minimum(sizes[giver] - 1, reach - sizes[sink]) // 2
    margin = jnp.where((giver == order[0]) | (sink == order[0]) | (sizes[sink] == 0), 0, jnp.maximum(margin, 0))
    moved = jax.random.randint(jax.random.fold_in(own, 4), (count // 2,), 0, 1 << 20) % (margin + 1)
    sizes = sizes.at[giver].add(-moved).at[sink].add(moved)
    labels = jnp.searchsorted(jnp.cumsum(sizes), jnp.arange(rows * top), side="right").astype(jnp.int32)
    listing = labels.reshape(top, rows).T
    listing = listing[jax.random.permutation(jax.random.fold_in(own, 1), rows)]
    turn = jax.random.randint(jax.random.fold_in(own, 2), (rows, 1), 0, top)
    return jnp.take_along_axis(listing, (jnp.arange(top)[None, :] + turn) % top, axis=1)


def portions_of(amount, total, reach, lean, full):
    portions = [(1 << 20) // math.isqrt(grade ** lean) + 1 for grade in range(1, amount + 1)]
    largest = reach if full else min(reach, max(-(-total // amount), total * portions[0] // sum(portions)))
    least = 1 if total - largest >= amount - 1 else 0
    holding, surplus = [largest] + [least] * (amount - 1), total - largest - least * (amount - 1)
    while surplus > 0:
        free = [i for i in range(1, amount) if holding[i] < largest] or [i for i in range(1, amount) if holding[i] < reach]
        mass, budget = sum([portions[i] for i in free]), surplus
        for i in free:
            extra = min(reach - holding[i], max(1, budget * portions[i] // mass), surplus)
            holding[i] = holding[i] + extra
            surplus = surplus - extra
    return np.array(holding)


def centred(stream_key, shape, scale, bound, split=(), kind=jnp.bfloat16):
    factor_of = block_scale(stream_key, shape, split, -0.22, 0.18) if split else 1.0
    array = jax.random.normal(stream_key, shape, jnp.float32) * scale * factor_of
    return jnp.minimum(jnp.maximum(array, -bound), bound).astype(kind)


def noise_with(key, extent, scale, reach, cuts, heavy, kind=jnp.bfloat16):
    result = scale * jax.random.normal(key, extent, jnp.float32)
    if cuts:
        result = result * block_scale(key, extent, cuts, -0.22, 0.18)
    return jnp.clip(with_spikes(result, jax.random.fold_in(key, 3), *heavy), -reach, reach).astype(kind)


def setup_inputs(seed: int = 0) -> dict:
    arg_keys = jax.random.split(jax.random.key(seed), 7)
    head_terms = noise_with(arg_keys[0], (TOKENS, HEADS, ROWS_H), TOKENS ** -0.5, 0.375, ((0, 4), (1, 8)), (0, 2, 4, 2.0))
    inputs = centred(arg_keys[1], (TOKENS, 2, D), 1.0, 6.0, ((0, 4),))
    owner_list_keys = jax.random.split(jax.random.fold_in(arg_keys[2], 1), HEADS * ROWS_H // BLOCK)
    owner_list_turns = jax.random.permutation(jax.random.fold_in(arg_keys[2], 3), HEADS * ROWS_H // BLOCK)
    owner_list = jax.vmap(lambda own, number: shared_out(jax.random.fold_in(arg_keys[2], 2), own, number, BLOCK, N_DP, 1, PAIR_MOST, 2))(owner_list_keys, owner_list_turns).reshape((HEADS, ROWS_H, 1))
    param_slots = centred(arg_keys[3], (HEADS, N_DP * SLOTS, D), 0.5, 3.0, ((0, 8), (1, 4)))
    row_state = jnp.clip(jnp.exp(math.log(4.0) - 2.7725887 * jax.random.uniform(arg_keys[4], (HEADS, N_DP * SLOTS), jnp.float32) ** block_scale(arg_keys[4], (HEADS, N_DP * SLOTS), ((0, 8), (1, 4)), -0.2, 0.2)), 0.25, 4.0)
    col_state = jnp.clip(jnp.exp(math.log(4.0) - 2.7725887 * jax.random.uniform(arg_keys[5], (HEADS, PROJ, D), jnp.float32) ** block_scale(arg_keys[5], (HEADS, PROJ, D), ((0, 8),), -0.2, 0.2)), 0.25, 4.0)
    return dict(head_terms=head_terms, inputs=inputs, owner_list=owner_list, param_slots=param_slots, row_state=row_state, col_state=col_state)


DECAY_RATE = 0.5
STEP_SIZE = 0.5
EPS_SQUARE = 1e-30

def slot_table(owner_col, owner_count, pair_most):
    row_count = owner_col.shape[0]
    block_rows = row_count // owner_count
    index_ids = jnp.arange(owner_count, dtype=jnp.int32)
    onehot = (owner_col[:, None] == index_ids[None, :]).astype(jnp.int32)
    blocked = onehot.reshape(owner_count, block_rows, owner_count)
    before = jnp.cumsum(blocked, axis=1) - blocked
    order_in = lax.optimization_barrier(jnp.sum(before * blocked, axis=2)).reshape(row_count)
    row_ids = jnp.arange(row_count, dtype=jnp.int32)
    block_of = row_ids // block_rows
    slot_ids = jnp.arange(pair_most, dtype=jnp.int32)
    match_owner = owner_col[None, None, None, :] == index_ids[:, None, None, None]
    match_block = block_of[None, None, None, :] == index_ids[None, :, None, None]
    match_slot = order_in[None, None, None, :] == slot_ids[None, None, :, None]
    hits = (match_owner & match_block & match_slot).astype(jnp.int32)
    live_mask = lax.optimization_barrier(jnp.sum(hits, axis=3)).reshape(owner_count, owner_count * pair_most)
    slot_row = lax.optimization_barrier(jnp.sum(hits * row_ids[None, None, None, :], axis=3)).reshape(owner_count, owner_count * pair_most)
    return (slot_row, live_mask)

def column_update(gradient, owner_col, params_col, rows_col, cols_col):
    slot_row, live_mask = slot_table(owner_col, N_DP, PAIR_MOST)
    flat_rows = slot_row.reshape(-1)
    live_f = live_mask.reshape(-1).astype(jnp.float32)
    grad_sq = gradient * gradient + EPS_SQUARE
    col_sum = lax.optimization_barrier(jnp.sum(grad_sq.reshape(PROJ, DKV, grad_sq.shape[1]), axis=1))
    new_col = DECAY_RATE * cols_col + (1.0 - DECAY_RATE) * col_sum / DKV
    row_sq = lax.optimization_barrier(jnp.mean(grad_sq, axis=1))
    row_val = DECAY_RATE * rows_col + (1.0 - DECAY_RATE) * jnp.take(row_sq, flat_rows)
    slot_pick = ((flat_rows // DKV)[:, None] == jnp.arange(PROJ, dtype=jnp.int32)[None, :]).astype(jnp.float32)
    row_mean = lax.optimization_barrier(jnp.sum(slot_pick * (row_val * live_f)[:, None], axis=0)) / DKV
    col_at = jnp.dot(slot_pick, new_col, precision=lax.Precision.HIGHEST)
    mean_at = lax.optimization_barrier(jnp.sum(slot_pick * row_mean[None, :], axis=1))
    second_moment = row_val[:, None] * col_at / mean_at[:, None]
    slot_grad = jnp.take(gradient, flat_rows, axis=0)
    update = slot_grad / jnp.sqrt(second_moment)
    new_param = ((params_col.astype(jnp.float32) - STEP_SIZE * update) * live_f[:, None]).astype(jnp.bfloat16)
    return (new_param, row_val * live_f, new_col)

def reference(head_terms, inputs, owner_list, param_slots, row_state, col_state):
    split_at = (PROJ - 1) * DKV

    def one_head(column_args):
        head_rows, owner_col, params_col, rows_col, cols_col = column_args
        first_part = jnp.dot(head_rows[:, :split_at].T, inputs[:, 0, :], preferred_element_type=jnp.float32)
        last_part = jnp.dot(head_rows[:, split_at:].T, inputs[:, 1, :], preferred_element_type=jnp.float32)
        gradient = jnp.concatenate([first_part, last_part], axis=0)
        return column_update(gradient, owner_col, params_col, rows_col, cols_col)
    new_params, new_rows, new_cols = lax.map(one_head, (jnp.transpose(head_terms, (1, 0, 2)), owner_list[:, :, 0], param_slots, row_state, col_state))
    return (new_params, new_rows, new_cols)
```

```python
import functools

import jax
import jax.numpy as jnp
from jax import lax
from jax.experimental import pallas as pl
from jax.experimental.pallas import tpu as pltpu
from jax.sharding import PartitionSpec as P

DKV = 64
PROJ = 4


DECAY_RATE = 0.5
STEP_SIZE = 0.5
EPS_SQUARE = 1e-30


def slot_table(owner_col, owner_count, pair_most):
    row_count = owner_col.shape[0]
    block_rows = row_count // owner_count
    index_ids = jnp.arange(owner_count, dtype=jnp.int32)
    onehot = (owner_col[:, None] == index_ids[None, :]).astype(jnp.int32)
    blocked = onehot.reshape(owner_count, block_rows, owner_count)
    before = jnp.cumsum(blocked, axis=1) - blocked
    order_in = jnp.sum(before * blocked, axis=2).reshape(row_count)
    row_ids = jnp.arange(row_count, dtype=jnp.int32)
    block_of = row_ids // block_rows
    slot_ids = jnp.arange(pair_most, dtype=jnp.int32)
    match_owner = owner_col[None, None, None, :] == index_ids[:, None, None, None]
    match_block = block_of[None, None, None, :] == index_ids[None, :, None, None]
    match_slot = order_in[None, None, None, :] == slot_ids[None, None, :, None]
    hits = (match_owner & match_block & match_slot).astype(jnp.int32)
    live_mask = jnp.sum(hits, axis=3).reshape(owner_count, owner_count * pair_most)
    slot_row = jnp.sum(hits * row_ids[None, None, None, :], axis=3).reshape(
        owner_count, owner_count * pair_most
    )
    return (slot_row, live_mask)


def general_step(head_terms, inputs, owner_list, param_slots, row_state, col_state):
    dp_count = lax.axis_size("dp")
    my_index = lax.axis_index("dp")
    head_rows = head_terms[:, 0, :]
    row_count = head_rows.shape[1]
    width = inputs.shape[2]
    slot_count = param_slots.shape[1]
    pair_most = slot_count // dp_count
    block_rows = row_count // dp_count
    split_at = (PROJ - 1) * DKV
    first_part = jnp.einsum(
        "tr,td->rd", head_rows[:, :split_at], inputs[:, 0, :], preferred_element_type=jnp.float32
    )
    last_part = jnp.einsum(
        "tr,td->rd", head_rows[:, split_at:], inputs[:, 1, :], preferred_element_type=jnp.float32
    )
    gradient = jnp.concatenate([first_part, last_part], axis=0)
    slot_row, live_mask = slot_table(owner_list[0, :, 0], dp_count, pair_most)
    home_sum = lax.psum_scatter(gradient, "dp", scatter_dimension=0, tiled=True)
    local_rows = (
        lax.dynamic_slice_in_dim(slot_row, my_index * pair_most, pair_most, 1)
        - my_index * block_rows
    )
    outgoing = jnp.take(home_sum, local_rows.reshape(-1), axis=0, mode="clip").reshape(
        dp_count, pair_most, width
    )
    received = lax.all_to_all(outgoing, "dp", split_axis=0, concat_axis=0, tiled=True)
    slot_grad = received.reshape(slot_count, width)
    my_rows = lax.dynamic_index_in_dim(slot_row, my_index, 0, keepdims=False)
    live_f = lax.dynamic_index_in_dim(live_mask, my_index, 0, keepdims=False).astype(jnp.float32)
    grad_sq = slot_grad * slot_grad + EPS_SQUARE
    row_val = DECAY_RATE * row_state[0] + (1.0 - DECAY_RATE) * jnp.mean(grad_sq, axis=1)
    slot_pick = ((my_rows // DKV)[:, None] == jnp.arange(PROJ, dtype=jnp.int32)[None, :]).astype(
        jnp.float32
    )
    live_pick = slot_pick * live_f[:, None]
    col_part = jnp.einsum("sp,sd->pd", live_pick, grad_sq, precision=lax.Precision.HIGHEST)
    row_part = jnp.sum(live_pick * row_val[:, None], axis=0)
    col_sum, row_total = lax.psum((col_part, row_part), "dp")
    new_col = DECAY_RATE * col_state[0] + (1.0 - DECAY_RATE) * col_sum / DKV
    row_mean = row_total / DKV
    col_at = jnp.dot(slot_pick, new_col, precision=lax.Precision.HIGHEST)
    mean_at = jnp.sum(slot_pick * row_mean[None, :], axis=1)
    second_moment = row_val[:, None] * col_at / mean_at[:, None]
    update = slot_grad / jnp.sqrt(second_moment)
    new_param = (
        (param_slots[0].astype(jnp.float32) - STEP_SIZE * update) * live_f[:, None]
    ).astype(jnp.bfloat16)
    return (new_param[None], (row_val * live_f)[None], new_col[None])


PIECES = 2
EXTRA = 8
BF16 = jnp.bfloat16
F32 = jnp.float32
VMEM_LIMIT = 48 * 1024 * 1024


def call(body, out_shape, scratch=(), scalars=1, arrays=0, flops=0, moved=0):
    return pl.pallas_call(
        body,
        out_shape=out_shape,
        in_specs=[pl.BlockSpec(memory_space=pltpu.SMEM)] * scalars
        + [pl.BlockSpec(memory_space=pltpu.VMEM)] * arrays,
        out_specs=jax.tree.map(lambda _: pl.BlockSpec(memory_space=pltpu.VMEM), out_shape),
        scratch_shapes=list(scratch),
        compiler_params=pltpu.CompilerParams(vmem_limit_bytes=VMEM_LIMIT),
        cost_estimate=pl.CostEstimate(flops=flops, bytes_accessed=moved, transcendentals=0),
    )


def iota(shape, dim):
    return lax.broadcasted_iota(jnp.int32, shape, dim)


def prepare(heads, rows, pair_most, place, *refs):
    first, later = refs[:heads], refs[heads : 2 * heads]
    split_ref, last_ref, live_ref, state_ref, total_ref = refs[2 * heads :]
    z = place[0]
    owners = rows // DKV
    block = rows // owners
    slots = owners * pair_most
    split, cut = rows - DKV, (owners - 1) * pair_most
    tokens = first[0].shape[1]
    half = rows // 2
    owner_rows = [
        jnp.concatenate([r[rows + 1 : rows + 2, :half], r[rows + 2 : rows + 3, :half]], axis=1)
        for r in first
    ]
    lane = iota((rows, rows), 1)
    row = iota((rows, rows), 0)
    earlier = ((row < lane) & (row // block == lane // block)).astype(F32).astype(BF16)
    named = jnp.concatenate(owner_rows + [jnp.full((8 - heads, rows), -1.0, F32)], axis=0)
    mine = named == z.astype(F32)
    before = jnp.dot(mine.astype(F32).astype(BF16), earlier, preferred_element_type=F32)
    at = iota((8, rows), 1) // block * pair_most
    slot_of = jnp.where(mine, before + at.astype(F32), -1.0)
    slot_id = iota((slots, rows), 0).astype(F32)
    all0, all1 = split + cut, rows - split + slots - cut
    for m in range(heads):
        terms = jnp.concatenate([first[m][:rows, :], later[m][:rows, :]], axis=1).astype(BF16)
        pick = (slot_id == slot_of[m : m + 1, :]).astype(F32)
        chosen = jnp.dot(pick.astype(BF16), terms, preferred_element_type=F32).astype(BF16)
        split_ref[m * all0 : m * all0 + split, :] = terms[:split]
        split_ref[m * all0 + split : (m + 1) * all0, :] = chosen[:cut]
        last_ref[m * all1 : m * all1 + rows - split, :] = terms[split:]
        last_ref[m * all1 + rows - split : (m + 1) * all1, :] = chosen[cut:]
        if m == 0:
            live_ref[...] = jnp.sum(pick, axis=1, keepdims=True)
    state = first[0][rows : rows + 1, :slots]
    same = iota((slots, slots), 0) == iota((slots, slots), 1)
    state_ref[...] = jnp.sum(jnp.where(same, state, 0.0), axis=1, keepdims=True)
    owner_of = jnp.where(iota((8, rows), 0) < owners, z ^ iota((8, rows), 0), -1).astype(F32)
    theirs = (owner_rows[0] == owner_of).astype(F32).astype(BF16)
    home = (iota((rows, slots), 0) // block == iota((rows, slots), 1) // pair_most).astype(F32)
    count = jnp.dot(theirs, home.astype(BF16), preferred_element_type=F32)
    held = (iota((8, slots), 1) % pair_most).astype(F32) < count
    states = [state] + [
        later[0][rows : rows + 1, k * tokens : k * tokens + slots] for k in range(owners - 1)
    ]
    states = jnp.concatenate(states + [jnp.zeros((8 - owners, slots), F32)], axis=0)
    states = jnp.where(held, states, 0.0)
    for i in range(owners):
        part = jnp.where(iota((8, slots), 1) // pair_most == i, states, 0.0)
        part = jnp.sum(jnp.sum(part, axis=1, keepdims=True), axis=0, keepdims=True)
        total_ref[i : i + 1, :] = jnp.broadcast_to(part, (1, slots))


def multiply(heads, split, cut, slots, place, split_terms, last_terms, *refs):
    own, near, one, two, mid, far, one_n, two_n, mid_n, far_n = refs[:10]
    outs, (held0, held1) = refs[10 : 10 + heads], refs[10 + heads :]
    tokens = own.shape[0] // 2
    half = own.shape[1]
    is_end = place[1] == 1

    def put(k, side, value):
        value = value.astype(BF16)
        held0[k * tokens : (k + 1) * tokens, side * half : (side + 1) * half] = value[:tokens]
        held1[k * tokens : (k + 1) * tokens, side * half : (side + 1) * half] = value[tokens:]

    put(0, 0, own[...])
    put(0, 1, near[...])
    put(1, 0, one[...])
    put(1, 1, one_n[...])
    put(2, 0, two[...])
    put(2, 1, two_n[...])
    put(3, 0, jnp.where(is_end, far[...], mid[...]))
    put(3, 1, jnp.where(is_end, far_n[...], mid_n[...]))
    x0, x1 = held0[...], held1[...]
    all0 = split + cut
    last = DKV
    all1 = last + slots - cut
    for m in range(heads):
        out = outs[m]
        g = jnp.dot(split_terms[m * all0 : (m + 1) * all0, :], x0, preferred_element_type=F32)
        out[:cut, :] = g[split:]
        for p in range(PROJ - 1):
            part = g[p * DKV : (p + 1) * DKV]
            out[slots + p : slots + p + 1, :] = jnp.sum(
                part * part + EPS_SQUARE, axis=0, keepdims=True
            )
        g = jnp.dot(last_terms[m * all1 : (m + 1) * all1, :], x1, preferred_element_type=F32)
        out[cut:slots, :] = g[last:]
        part = g[:last]
        out[slots + PROJ - 1 : slots + PROJ, :] = jnp.sum(
            part * part + EPS_SQUARE, axis=0, keepdims=True
        )


def update(heads, pieces, pair_most, place, *refs):
    grads, refs = refs[: heads * pieces], refs[heads * pieces :]
    params, live_ref, state_ref, total_ref, cols, new_params, new_rows, new_cols = refs
    chip, core = place[2], place[3]
    slots, width = params.shape
    piece = grads[0].shape[1]
    half = piece // 2
    square = jnp.zeros((slots, 128), F32)
    sums = jnp.zeros((PROJ, 128), F32)
    spans = []
    for m in range(heads):
        for p in range(pieces):
            ref = grads[m * pieces + p]
            for side in range(2):
                start = (chip ^ m) * (width // heads) + p * piece + (core ^ side) * half
                spans.append((ref, side * half, pl.multiple_of(start, 128)))
    for ref, lo, start in spans:
        for j in range(0, half, 128):
            g = ref[:slots, lo + j : lo + j + 128]
            square += g * g + EPS_SQUARE
        col_sum = ref[slots : slots + PROJ, lo : lo + half]
        for j in range(0, half, 128):
            sums += col_sum[:, j : j + 128]
        new_cols[:, pl.ds(start, half)] = (
            DECAY_RATE * cols[:, pl.ds(start, half)] + (1.0 - DECAY_RATE) * col_sum / DKV
        )
    row_val = DECAY_RATE * state_ref[...] + (1.0 - DECAY_RATE) * (
        jnp.sum(square, axis=1, keepdims=True) / width
    )
    row_mean = (
        DECAY_RATE * total_ref[:, :1]
        + (1.0 - DECAY_RATE) * jnp.sum(sums, axis=1, keepdims=True) / width
    ) / DKV
    mean_at = jnp.concatenate(
        [jnp.broadcast_to(row_mean[i : i + 1], (pair_most, 1)) for i in range(PROJ)], axis=0
    )
    live = live_ref[...]
    row_scale = STEP_SIZE * jnp.sqrt(mean_at / row_val)
    same = iota((slots, slots), 0) == iota((slots, slots), 1)
    new_rows[...] = jnp.sum(jnp.where(same, row_val * live, 0.0), axis=0, keepdims=True)
    for ref, lo, start in spans:
        col_scale = lax.rsqrt(new_cols[:, pl.ds(start, half)])
        for i in range(PROJ):
            rows = slice(i * pair_most, (i + 1) * pair_most)
            step = ref[rows, lo : lo + half] * row_scale[rows] * col_scale[i : i + 1]
            value = params[rows, pl.ds(start, half)].astype(F32) - step
            new_params[rows, pl.ds(start, half)] = jnp.where(live[rows] > 0.0, value, 0.0).astype(
                BF16
            )


def gather_step(
    dp_count, shard_count, head_terms, inputs, owner_list, param_slots, row_state, col_state
):
    z, s = lax.axis_index("dp"), lax.axis_index("shard")
    chip, core = s // 2, s % 2
    is_end = ((z == 0) | (z == dp_count - 1)).astype(jnp.int32)
    place = jnp.stack([z, is_end, chip, core]).astype(jnp.int32)
    heads = shard_count // 2
    tokens, _, width = inputs.shape
    rows = head_terms.shape[2]
    slots = param_slots.shape[1]
    pair_most = slots // dp_count
    span = width // heads
    piece = span // PIECES
    half = piece // 2
    split, cut = rows - DKV, slots - pair_most

    def move(array, dp_to, shard_to=lambda j: j):
        pairs = [
            (i * shard_count + j, dp_to[i] * shard_count + shard_to(j))
            for i in dp_to
            for j in range(shard_count)
        ]
        return lax.ppermute(array, ("dp", "shard"), pairs)

    every = {i: i for i in range(4)}
    ends, inner = {0: 0, 3: 3}, {1: 1, 2: 2}

    def along(array):
        two = move(array, {i: i ^ 2 for i in range(4)})
        one = move(array, {i: i ^ 1 for i in range(4)})
        mid = move(array, {1: 2, 2: 1})
        far = move(two, {1: 0, 2: 3})
        return one, two, mid, far

    def across(array):
        return [move(array, every, lambda j, m=m: j ^ (2 * m)) for m in range(1, heads)]

    extra = jnp.concatenate(
        [
            row_state,
            owner_list[0, :, 0].astype(F32).reshape(2, rows // 2),
            jnp.zeros((EXTRA - 3, tokens), F32),
        ],
        axis=0,
    )
    terms = jnp.concatenate([head_terms[:, 0, :].T.astype(F32), extra], axis=0)
    mine = lax.dynamic_slice_in_dim(inputs, chip * span, span, 2)

    def columns(start):
        part = lax.dynamic_slice_in_dim(mine, start, half, 2)
        return part.transpose(1, 0, 2).reshape(2 * tokens, half).astype(F32)

    own = [columns(p * piece + core * half) for p in range(PIECES)]
    near = [columns(p * piece + (1 - core) * half) for p in range(PIECES)]

    one, two, mid, far = along(terms)
    later = jnp.concatenate([one, two, jnp.where(is_end == 1, far, mid)], axis=1)
    first_all = [terms] + across(terms)
    later_all = [later] + across(later)
    depth = dp_count * tokens
    split_terms, last_terms, live, state, total = call(
        functools.partial(prepare, heads, rows, pair_most),
        [
            jax.ShapeDtypeStruct((heads * (split + cut), depth), BF16),
            jax.ShapeDtypeStruct((heads * (rows - split + slots - cut), depth), BF16),
            jax.ShapeDtypeStruct((slots, 1), F32),
            jax.ShapeDtypeStruct((slots, 1), F32),
            jax.ShapeDtypeStruct((PROJ, slots), F32),
        ],
        arrays=2 * heads,
        flops=2 * heads * slots * rows * depth,
        moved=8 * heads * rows * depth,
    )(place, *first_all, *later_all)

    grads = []
    for p in range(PIECES):
        one, two, mid, far = along(own[p])
        swap = lambda j: j ^ 1
        one_n, two_n = move(one, every, swap), move(two, every, swap)
        mid_n, far_n = move(mid, inner, swap), move(far, ends, swap)
        outs = call(
            functools.partial(multiply, heads, split, cut, slots),
            [jax.ShapeDtypeStruct((slots + EXTRA, piece), F32)] * heads,
            scratch=[pltpu.VMEM((depth, piece), BF16)] * 2,
            arrays=12,
            flops=2 * heads * (rows + slots) * depth * piece,
            moved=8 * depth * piece,
        )(place, split_terms, last_terms, own[p], near[p], one, two, mid, far, one_n, two_n, mid_n, far_n)
        grads.append(
            [outs[0]] + [move(outs[m], every, lambda j, m=m: j ^ (2 * m)) for m in range(1, heads)]
        )
    flat = [grads[p][m] for m in range(heads) for p in range(PIECES)]
    new_params, new_rows, new_cols = call(
        functools.partial(update, heads, PIECES, pair_most),
        [
            jax.ShapeDtypeStruct((slots, width), BF16),
            jax.ShapeDtypeStruct((1, slots), F32),
            jax.ShapeDtypeStruct((PROJ, width), F32),
        ],
        arrays=len(flat) + 5,
        moved=4 * slots * width * 2,
    )(place, *flat, param_slots[0], live, state, total, col_state[0])
    return (new_params[None], new_rows, new_cols[None])


def one_step(mesh, *args):
    dp_count, shard_count = mesh.shape["dp"], mesh.shape["shard"]
    if dp_count == 4 and shard_count == 8:
        return gather_step(dp_count, shard_count, *args)
    return general_step(*args)


def solution(mesh):
    placed = (
        P("dp", "shard", None),
        P("dp", None, None),
        P("shard", None, None),
        P("shard", "dp", None),
        P("shard", "dp"),
        P("shard", None, None),
    )
    return jax.shard_map(
        functools.partial(one_step, mesh),
        mesh=mesh,
        in_specs=placed,
        out_specs=(P("shard", "dp", None), P("shard", "dp"), P("shard", None, None)),
        check_vma=False,
    )
```

```python
import functools

import jax
import jax.numpy as jnp
from jax import lax
from jax.experimental import pallas as pl
from jax.experimental.pallas import tpu as pltpu
from jax.sharding import PartitionSpec as P

DKV = 64
PROJ = 4


DECAY_RATE = 0.5
STEP_SIZE = 0.5
EPS_SQUARE = 1e-30


def slot_table(owner_col, owner_count, pair_most):
    row_count = owner_col.shape[0]
    block_rows = row_count // owner_count
    index_ids = jnp.arange(owner_count, dtype=jnp.int32)
    onehot = (owner_col[:, None] == index_ids[None, :]).astype(jnp.int32)
    blocked = onehot.reshape(owner_count, block_rows, owner_count)
    before = jnp.cumsum(blocked, axis=1) - blocked
    order_in = jnp.sum(before * blocked, axis=2).reshape(row_count)
    row_ids = jnp.arange(row_count, dtype=jnp.int32)
    block_of = row_ids // block_rows
    slot_ids = jnp.arange(pair_most, dtype=jnp.int32)
    match_owner = owner_col[None, None, None, :] == index_ids[:, None, None, None]
    match_block = block_of[None, None, None, :] == index_ids[None, :, None, None]
    match_slot = order_in[None, None, None, :] == slot_ids[None, None, :, None]
    hits = (match_owner & match_block & match_slot).astype(jnp.int32)
    live_mask = jnp.sum(hits, axis=3).reshape(owner_count, owner_count * pair_most)
    slot_row = jnp.sum(hits * row_ids[None, None, None, :], axis=3).reshape(
        owner_count, owner_count * pair_most
    )
    return (slot_row, live_mask)


def general_step(head_terms, inputs, owner_list, param_slots, row_state, col_state):
    dp_count = lax.axis_size("dp")
    my_index = lax.axis_index("dp")
    head_rows = head_terms[:, 0, :]
    row_count = head_rows.shape[1]
    width = inputs.shape[2]
    slot_count = param_slots.shape[1]
    pair_most = slot_count // dp_count
    block_rows = row_count // dp_count
    split_at = (PROJ - 1) * DKV
    first_part = jnp.einsum(
        "tr,td->rd", head_rows[:, :split_at], inputs[:, 0, :], preferred_element_type=jnp.float32
    )
    last_part = jnp.einsum(
        "tr,td->rd", head_rows[:, split_at:], inputs[:, 1, :], preferred_element_type=jnp.float32
    )
    gradient = jnp.concatenate([first_part, last_part], axis=0)
    slot_row, live_mask = slot_table(owner_list[0, :, 0], dp_count, pair_most)
    home_sum = lax.psum_scatter(gradient, "dp", scatter_dimension=0, tiled=True)
    local_rows = (
        lax.dynamic_slice_in_dim(slot_row, my_index * pair_most, pair_most, 1)
        - my_index * block_rows
    )
    outgoing = jnp.take(home_sum, local_rows.reshape(-1), axis=0, mode="clip").reshape(
        dp_count, pair_most, width
    )
    received = lax.all_to_all(outgoing, "dp", split_axis=0, concat_axis=0, tiled=True)
    slot_grad = received.reshape(slot_count, width)
    my_rows = lax.dynamic_index_in_dim(slot_row, my_index, 0, keepdims=False)
    live_f = lax.dynamic_index_in_dim(live_mask, my_index, 0, keepdims=False).astype(jnp.float32)
    grad_sq = slot_grad * slot_grad + EPS_SQUARE
    row_val = DECAY_RATE * row_state[0] + (1.0 - DECAY_RATE) * jnp.mean(grad_sq, axis=1)
    slot_pick = ((my_rows // DKV)[:, None] == jnp.arange(PROJ, dtype=jnp.int32)[None, :]).astype(
        jnp.float32
    )
    live_pick = slot_pick * live_f[:, None]
    col_part = jnp.einsum("sp,sd->pd", live_pick, grad_sq, precision=lax.Precision.HIGHEST)
    row_part = jnp.sum(live_pick * row_val[:, None], axis=0)
    col_sum, row_total = lax.psum((col_part, row_part), "dp")
    new_col = DECAY_RATE * col_state[0] + (1.0 - DECAY_RATE) * col_sum / DKV
    row_mean = row_total / DKV
    col_at = jnp.dot(slot_pick, new_col, precision=lax.Precision.HIGHEST)
    mean_at = jnp.sum(slot_pick * row_mean[None, :], axis=1)
    second_moment = row_val[:, None] * col_at / mean_at[:, None]
    update = slot_grad / jnp.sqrt(second_moment)
    new_param = (
        (param_slots[0].astype(jnp.float32) - STEP_SIZE * update) * live_f[:, None]
    ).astype(jnp.bfloat16)
    return (new_param[None], (row_val * live_f)[None], new_col[None])


EXTRA = 8
CFG = dict(c0=0, c1=1e10, pr=4e10, m0=0, m1=0, ea=0, e=(1, 2), s1=0, s2=0)
BF16 = jnp.bfloat16
F32 = jnp.float32
VMEM_LIMIT = 16 * 1024 * 1024
BEGIN_LIMIT = 56 * 1024 * 1024


def here_of():
    s = lax.axis_index("shard")
    return lax.axis_index("dp"), s // 2, s % 2


def call(body, out_shape, scratch=(), arrays=0, flops=0, moved=0):
    return pl.pallas_call(
        body,
        out_shape=out_shape,
        in_specs=[pl.BlockSpec(memory_space=pltpu.VMEM)] * arrays,
        out_specs=jax.tree.map(lambda _: pl.BlockSpec(memory_space=pltpu.VMEM), out_shape),
        scratch_shapes=list(scratch),
        compiler_params=pltpu.CompilerParams(vmem_limit_bytes=VMEM_LIMIT),
        cost_estimate=pl.CostEstimate(flops=flops, bytes_accessed=moved, transcendentals=0),
    )


def iota(shape, dim):
    return lax.broadcasted_iota(jnp.int32, shape, dim)


def begin(rows, heads_hbm, owner_hbm, state_hbm, terms_ref, heads_ref, owner_ref, state_ref, sems):
    copies = [
        pltpu.make_async_copy(heads_hbm, heads_ref, sems.at[0]),
        pltpu.make_async_copy(owner_hbm, owner_ref, sems.at[1]),
        pltpu.make_async_copy(state_hbm, state_ref, sems.at[2]),
    ]
    for copy in copies:
        copy.start()
    for copy in copies:
        copy.wait()
    terms_ref[:rows, :] = heads_ref[...].astype(F32).T
    terms_ref[rows : rows + 1, :] = state_ref[...]
    named = owner_ref[...].astype(F32)
    terms_ref[rows + 1 : rows + 2, :] = named[:, : rows // 2]
    terms_ref[rows + 2 : rows + 3, :] = named[:, rows // 2 :]
    terms_ref[rows + 3 :, :] = jnp.zeros((terms_ref.shape[0] - rows - 3, terms_ref.shape[1]), F32)


def columns(inputs_hbm, *refs):
    *outs, inputs_ref, sem = refs
    _, chip, core = here_of()
    half = outs[0].shape[1]
    span = 2 * half
    some = pl.ds(pl.multiple_of(chip * span, 128), span)
    copy = pltpu.make_async_copy(inputs_hbm.at[:, :, some], inputs_ref, sem)
    copy.start()
    copy.wait()
    for c in range(2):
        for side in range(2):
            at = pl.multiple_of((core ^ side) * half, 128)
            outs[2 * c + side][...] = inputs_ref[:, c, pl.ds(at, half)].astype(F32)


def spread(*refs):
    *blocks, out_ref = refs
    at = 0
    for block in blocks:
        value = block[...]
        for j in range(out_ref.shape[0]):
            out_ref[j, :, at : at + value.shape[1]] = value
        at += value.shape[1]


def collect(up1, down1, up2, down2, up3, down3, out_ref):
    z, _, _ = here_of()
    tokens = up1.shape[0]
    out_ref[:tokens, :] = jnp.where(z >= 1, up1[...], down3[...])
    out_ref[tokens : 2 * tokens, :] = jnp.where(z <= 2, down1[...], up3[...])
    out_ref[2 * tokens :, :] = jnp.where(z <= 1, down2[...], up2[...])


def prepare(heads, rows, pair_most, *refs):
    *parts, split_ref, last_ref, live_ref, state_ref, total_ref = refs
    z, chip, _ = here_of()
    owners = rows // DKV
    tokens = sum(part.shape[2] for part in parts) // owners
    block = rows // owners
    slots = owners * pair_most
    split, cut = rows - DKV, (owners - 1) * pair_most
    half = rows // 2

    def owner_row(m):
        at = chip ^ m
        return jnp.concatenate(
            [parts[0][at, rows + 1 : rows + 2, :half], parts[0][at, rows + 2 : rows + 3, :half]], axis=1
        )

    lane = iota((rows, rows), 1)
    row = iota((rows, rows), 0)
    earlier = ((row < lane) & (row // block == lane // block)).astype(F32).astype(BF16)
    named = jnp.concatenate(
        [owner_row(m) for m in range(heads)] + [jnp.full((8 - heads, rows), -1.0, F32)], axis=0
    )
    mine = named == z.astype(F32)
    before = jnp.dot(mine.astype(F32).astype(BF16), earlier, preferred_element_type=F32)
    at = iota((8, rows), 1) // block * pair_most
    slot_of = jnp.where(mine, before + at.astype(F32), -1.0)
    slot_id = iota((slots, rows), 0).astype(F32)
    all0, all1 = split + cut, rows - split + slots - cut
    for m in range(heads):
        terms = jnp.concatenate([part[chip ^ m, :rows, :] for part in parts], axis=1).astype(BF16)
        pick = (slot_id == slot_of[m : m + 1, :]).astype(F32)
        chosen = jnp.dot(pick.astype(BF16), terms, preferred_element_type=F32).astype(BF16)
        split_ref[m * all0 : m * all0 + split, :] = terms[:split]
        split_ref[m * all0 + split : (m + 1) * all0, :] = chosen[:cut]
        last_ref[m * all1 : m * all1 + rows - split, :] = terms[split:]
        last_ref[m * all1 + rows - split : (m + 1) * all1, :] = chosen[cut:]
        if m == 0:
            live_ref[...] = jnp.sum(pick, axis=1, keepdims=True)
    state = parts[0][chip, rows : rows + 1, :slots]
    same = iota((slots, slots), 0) == iota((slots, slots), 1)
    state_ref[...] = jnp.sum(jnp.where(same, state, 0.0), axis=1, keepdims=True)
    owner_of = jnp.where(
        iota((8, rows), 0) == 0,
        z,
        jnp.where(
            iota((8, rows), 0) == 1,
            (z + owners - 1) % owners,
            jnp.where(iota((8, rows), 0) == 2, (z + 1) % owners, (z + 2) % owners),
        ),
    ).astype(F32)
    theirs = (owner_row(0) == owner_of).astype(F32).astype(BF16)
    home = (iota((rows, slots), 0) // block == iota((rows, slots), 1) // pair_most).astype(F32)
    count = jnp.dot(theirs, home.astype(BF16), preferred_element_type=F32)
    held = (iota((8, slots), 1) % pair_most).astype(F32) < count
    states = [
        part[chip, rows : rows + 1, k : k + slots]
        for part in parts
        for k in range(0, part.shape[2], tokens)
    ]
    states = jnp.concatenate(states + [jnp.zeros((8 - owners, slots), F32)], axis=0)
    states = jnp.where(held, states, 0.0)
    for i in range(owners):
        part = jnp.where(iota((8, slots), 1) // pair_most == i, states, 0.0)
        part = jnp.sum(jnp.sum(part, axis=1, keepdims=True), axis=0, keepdims=True)
        total_ref[i : i + 1, :] = jnp.broadcast_to(part, (1, slots))


def multiply(heads, projections, slots, terms, own, near, here, there, *refs):
    *refs, held = refs
    sums_ref, outs = (refs[-1], refs[:-1]) if projections > 1 else (refs[0], refs[1:])
    tokens, half = own.shape
    sides = [
        [own[...]] + [here[k * tokens : (k + 1) * tokens, :] for k in range(3)],
        [near[...]] + [there[k * tokens : (k + 1) * tokens, :] for k in range(3)],
    ]
    for side, values in enumerate(sides):
        for k, value in enumerate(values):
            held[k * tokens : (k + 1) * tokens, side * half : (side + 1) * half] = value.astype(BF16)
    x = held[...]
    each = projections * DKV + slots
    for m in range(heads):
        g = jnp.dot(terms[m * each : (m + 1) * each, :], x, preferred_element_type=F32)
        outs[m][:slots, :] = g[projections * DKV :]
        for p in range(projections):
            part = g[p * DKV : (p + 1) * DKV]
            sums = jnp.sum(part * part + EPS_SQUARE, axis=0, keepdims=True)
            if projections > 1:
                sums_ref[m, p : p + 1, :] = sums
            else:
                outs[m][slots + PROJ - 1 : slots + PROJ, :] = sums
        if projections == 1:
            outs[m][slots : slots + PROJ - 1, :] = sums_ref[m, : PROJ - 1, :]


def spans_of(refs, width):
    _, chip, core = here_of()
    heads = len(refs)
    span = width // heads
    half = span // 2
    return [
        (refs[m], side * half, pl.multiple_of((chip ^ m) * span + (core ^ side) * half, 128))
        for m in range(heads)
        for side in range(2)
    ], half


def squares(refs, count):
    square = jnp.zeros((count, 128), F32)
    for ref in refs:
        for j in range(0, ref.shape[1], 128):
            g = ref[:count, j : j + 128]
            square += g * g + EPS_SQUARE
    return jnp.sum(square, axis=1, keepdims=True)


def early(*refs):
    *first, square_ref = refs
    square_ref[...] = squares(first, square_ref.shape[0])


def update(heads, pair_most, *refs):
    first, last, refs = refs[:heads], refs[heads : 2 * heads], refs[2 * heads :]
    square0, params, live_ref, state_ref, total_ref, cols, new_params, new_rows, new_cols = refs
    slots, width = params.shape
    cut = (PROJ - 1) * pair_most
    rest = slots - cut
    sums = jnp.zeros((PROJ, 128), F32)
    spans, half = spans_of(last, width)
    for ref, lo, start in spans:
        col_sum = ref[rest : rest + PROJ, lo : lo + half]
        for j in range(0, half, 128):
            sums += col_sum[:, j : j + 128]
        new_cols[:, pl.ds(start, half)] = (
            DECAY_RATE * cols[:, pl.ds(start, half)] + (1.0 - DECAY_RATE) * col_sum / DKV
        )
    square = jnp.concatenate([square0[...], squares(last, rest)], axis=0)
    row_val = DECAY_RATE * state_ref[...] + (1.0 - DECAY_RATE) * (square / width)
    row_mean = (
        DECAY_RATE * total_ref[:, :1]
        + (1.0 - DECAY_RATE) * jnp.sum(sums, axis=1, keepdims=True) / width
    ) / DKV
    mean_at = jnp.concatenate(
        [jnp.broadcast_to(row_mean[i : i + 1], (pair_most, 1)) for i in range(PROJ)], axis=0
    )
    live = live_ref[...]
    row_scale = STEP_SIZE * jnp.sqrt(mean_at / row_val)
    same = iota((slots, slots), 0) == iota((slots, slots), 1)
    new_rows[...] = jnp.sum(jnp.where(same, row_val * live, 0.0), axis=0, keepdims=True)
    for m, (_, lo, start) in zip([m for m in range(heads) for _ in range(2)], spans):
        col_scale = lax.rsqrt(new_cols[:, pl.ds(start, half)])
        for i in range(PROJ):
            rows = slice(i * pair_most, (i + 1) * pair_most)
            ref, k = (first[m], i) if i < PROJ - 1 else (last[m], 0)
            g = ref[k * pair_most : (k + 1) * pair_most, lo : lo + half]
            value = params[rows, pl.ds(start, half)].astype(F32) - g * row_scale[rows] * (
                col_scale[i : i + 1]
            )
            new_params[rows, pl.ds(start, half)] = jnp.where(live[rows] > 0.0, value, 0.0).astype(
                BF16
            )


def gather_step(
    dp_count, shard_count, head_terms, inputs, owner_list, param_slots, row_state, col_state
):
    heads = shard_count // 2
    tokens, _, width = inputs.shape
    rows = head_terms.shape[2]
    slots = param_slots.shape[1]
    pair_most = slots // dp_count
    span = width // heads
    half = span // 2
    split, cut = rows - DKV, slots - pair_most
    depth = dp_count * tokens

    def move(array, dp_to, shard_to=lambda j: j):
        pairs = [
            (i * shard_count + j, dp_to[i] * shard_count + shard_to(j))
            for i in dp_to
            for j in range(shard_count)
        ]
        return lax.ppermute(array, ("dp", "shard"), pairs)

    every = {i: i for i in range(4)}
    upward, downward = {i: i + 1 for i in range(3)}, {i + 1: i for i in range(3)}
    swap = lambda j: j ^ 1

    anywhere = pl.BlockSpec(memory_space=pl.ANY)
    in_vmem = pl.BlockSpec(memory_space=pltpu.VMEM)
    terms = pl.pallas_call(
        functools.partial(begin, rows),
        out_shape=jax.ShapeDtypeStruct((rows + EXTRA, tokens), F32),
        in_specs=[anywhere] * 3,
        out_specs=in_vmem,
        scratch_shapes=[
            pltpu.VMEM((tokens, rows), BF16),
            pltpu.VMEM((1, rows), jnp.int32),
            pltpu.VMEM((1, tokens), F32),
            pltpu.SemaphoreType.DMA((3,)),
        ],
        compiler_params=pltpu.CompilerParams(vmem_limit_bytes=BEGIN_LIMIT),
    )(head_terms[:, 0, :], owner_list[:, :, 0], row_state)
    own0, near0, own1, near1 = pl.pallas_call(
        columns,
        out_shape=[jax.ShapeDtypeStruct((tokens, half), F32)] * 4,
        in_specs=[anywhere],
        out_specs=[in_vmem] * 4,
        scratch_shapes=[pltpu.VMEM((tokens, 2, span), BF16), pltpu.SemaphoreType.DMA(())],
        compiler_params=pltpu.CompilerParams(vmem_limit_bytes=BEGIN_LIMIT),
    )(inputs)

    def after(array, *others):
        return lax.optimization_barrier((array, *others))[0] if others else array

    chips = [[2 * i + c for i in range(heads)] for c in range(2)]
    ring = lambda k: {i: (i + k) % dp_count for i in range(dp_count)}
    edges = CFG["e"]

    def edge(k, array, *others):
        return after(array, *others) if k in edges else array

    def exchange(*blocks):
        size = sum(block.shape[1] for block in blocks)
        everywhere = call(
            spread,
            jax.ShapeDtypeStruct((heads, rows + EXTRA, size), F32),
            arrays=len(blocks),
        )(*blocks)
        return lax.all_to_all(everywhere, "shard", 0, 0, axis_index_groups=chips)

    def joined(cost, *arrays):
        here = call(
            collect,
            jax.ShapeDtypeStruct((3 * tokens, half), F32),
            arrays=6,
            flops=int(cost),
        )(*arrays)
        return here, move(here, every, swap)

    def product(cost, terms, projections, count, *blocks):
        shapes = [jax.ShapeDtypeStruct((count if projections > 1 else count + EXTRA, span), F32)] * heads
        if projections > 1:
            shapes.append(jax.ShapeDtypeStruct((heads, 8, span), F32))
        return call(
            functools.partial(multiply, heads, projections, count),
            shapes,
            scratch=[pltpu.VMEM((depth, span), BF16)],
            arrays=1 + len(blocks),
            flops=int(cost),
        )(terms, *blocks)

    def scatter(outs):
        return [
            out if m == 0 else move(out, every, lambda j, m=m: j ^ (2 * m))
            for m, out in enumerate(outs)
        ]

    up1, down1 = move(own0, upward), move(own0, downward)
    ha, hb, hc = [move(terms, ring(k)) for k in (1, dp_count - 1, 2)]
    if CFG["s1"] == 0:
        parts = [exchange(terms, ha, hb, edge(3, hc, up1, down1))]
    elif CFG["s1"] == 1:
        parts = [exchange(terms, ha, hb)]
        parts.append(exchange(edge(3, hc, up1, down1)))
    elif CFG["s1"] == 2:
        parts = [exchange(terms)]
        parts.append(exchange(ha, hb, edge(3, edge(11, hc, parts[0]), up1, down1)))
    else:
        parts = [exchange(terms, ha)]
        parts.append(exchange(hb, edge(3, hc, up1, down1)))
    up2, down2 = move(edge(1, up1, ha), upward), move(edge(1, down1, hb), downward)
    x1 = edge(5, edge(2, own1, hc), up1, down1)
    x1 = edge(12, x1, up2, down2)
    nup1, ndown1 = move(x1, upward), move(x1, downward)
    up3 = move(edge(4, up2, nup1), upward)
    down3 = move(edge(4, down2, ndown1), downward)
    here0, there0 = joined(CFG["c0"], up1, down1, up2, down2, up3, down3)
    nup2, ndown2 = move(edge(6, nup1, up2), upward), move(edge(6, ndown1, down2), downward)
    parts[0] = edge(13, parts[0], there0)
    split_terms, last_terms, live, state, total = call(
        functools.partial(prepare, heads, rows, pair_most),
        [
            jax.ShapeDtypeStruct((heads * (split + cut), depth), BF16),
            jax.ShapeDtypeStruct((heads * (rows - split + slots - cut), depth), BF16),
            jax.ShapeDtypeStruct((slots, 1), F32),
            jax.ShapeDtypeStruct((slots, 1), F32),
            jax.ShapeDtypeStruct((PROJ, slots), F32),
        ],
        arrays=len(parts),
        flops=int(CFG["pr"]),
    )(*parts)
    here0 = edge(9, here0, nup2, ndown2)
    *outs, sums0 = product(CFG["m0"], split_terms, PROJ - 1, cut, own0, near0, here0, there0)
    first = scatter(outs)
    nup3 = move(edge(14, edge(7, nup2, outs[0]), there0), upward)
    ndown3 = move(edge(14, edge(7, ndown2, outs[0]), there0), downward)
    nup1 = edge(10, edge(8, nup1, first[1]), outs[0])
    here1, there1 = joined(CFG["c1"], nup1, ndown1, nup2, ndown2, nup3, ndown3)
    last = scatter(
        product(CFG["m1"], last_terms, 1, slots - cut, own1, near1, here1, there1, sums0)
    )
    square0 = call(
        early,
        jax.ShapeDtypeStruct((cut, 1), F32),
        arrays=heads,
        flops=int(CFG["ea"]),
    )(*first)
    new_params, new_rows, new_cols = call(
        functools.partial(update, heads, pair_most),
        [
            jax.ShapeDtypeStruct((slots, width), BF16),
            jax.ShapeDtypeStruct((1, slots), F32),
            jax.ShapeDtypeStruct((PROJ, width), F32),
        ],
        arrays=2 * heads + 6,
        moved=4 * slots * width * 2,
    )(*first, *last, square0, param_slots[0], live, state, total, col_state[0])
    return (new_params[None], new_rows, new_cols[None])


def one_step(mesh, *args):
    dp_count, shard_count = mesh.shape["dp"], mesh.shape["shard"]
    if dp_count == 4 and shard_count == 8:
        return gather_step(dp_count, shard_count, *args)
    return general_step(*args)


def solution(mesh):
    placed = (
        P("dp", "shard", None),
        P("dp", None, None),
        P("shard", None, None),
        P("shard", "dp", None),
        P("shard", "dp"),
        P("shard", None, None),
    )
    return jax.shard_map(
        functools.partial(one_step, mesh),
        mesh=mesh,
        in_specs=placed,
        out_specs=(P("shard", "dp", None), P("shard", "dp"), P("shard", None, None)),
        check_vma=False,
    )
```

```python
import functools

import jax
import jax.numpy as jnp
from jax import lax
from jax.experimental import pallas as pl
from jax.experimental.pallas import tpu as pltpu
from jax.sharding import PartitionSpec as P

DKV = 64
PROJ = 4


DECAY_RATE = 0.5
STEP_SIZE = 0.5
EPS_SQUARE = 1e-30


def slot_table(owner_col, owner_count, pair_most):
    row_count = owner_col.shape[0]
    block_rows = row_count // owner_count
    index_ids = jnp.arange(owner_count, dtype=jnp.int32)
    onehot = (owner_col[:, None] == index_ids[None, :]).astype(jnp.int32)
    blocked = onehot.reshape(owner_count, block_rows, owner_count)
    before = jnp.cumsum(blocked, axis=1) - blocked
    order_in = jnp.sum(before * blocked, axis=2).reshape(row_count)
    row_ids = jnp.arange(row_count, dtype=jnp.int32)
    block_of = row_ids // block_rows
    slot_ids = jnp.arange(pair_most, dtype=jnp.int32)
    match_owner = owner_col[None, None, None, :] == index_ids[:, None, None, None]
    match_block = block_of[None, None, None, :] == index_ids[None, :, None, None]
    match_slot = order_in[None, None, None, :] == slot_ids[None, None, :, None]
    hits = (match_owner & match_block & match_slot).astype(jnp.int32)
    live_mask = jnp.sum(hits, axis=3).reshape(owner_count, owner_count * pair_most)
    slot_row = jnp.sum(hits * row_ids[None, None, None, :], axis=3).reshape(
        owner_count, owner_count * pair_most
    )
    return (slot_row, live_mask)


def general_step(head_terms, inputs, owner_list, param_slots, row_state, col_state):
    dp_count = lax.axis_size("dp")
    my_index = lax.axis_index("dp")
    head_rows = head_terms[:, 0, :]
    row_count = head_rows.shape[1]
    width = inputs.shape[2]
    slot_count = param_slots.shape[1]
    pair_most = slot_count // dp_count
    block_rows = row_count // dp_count
    split_at = (PROJ - 1) * DKV
    first_part = jnp.einsum(
        "tr,td->rd", head_rows[:, :split_at], inputs[:, 0, :], preferred_element_type=jnp.float32
    )
    last_part = jnp.einsum(
        "tr,td->rd", head_rows[:, split_at:], inputs[:, 1, :], preferred_element_type=jnp.float32
    )
    gradient = jnp.concatenate([first_part, last_part], axis=0)
    slot_row, live_mask = slot_table(owner_list[0, :, 0], dp_count, pair_most)
    home_sum = lax.psum_scatter(gradient, "dp", scatter_dimension=0, tiled=True)
    local_rows = (
        lax.dynamic_slice_in_dim(slot_row, my_index * pair_most, pair_most, 1)
        - my_index * block_rows
    )
    outgoing = jnp.take(home_sum, local_rows.reshape(-1), axis=0, mode="clip").reshape(
        dp_count, pair_most, width
    )
    received = lax.all_to_all(outgoing, "dp", split_axis=0, concat_axis=0, tiled=True)
    slot_grad = received.reshape(slot_count, width)
    my_rows = lax.dynamic_index_in_dim(slot_row, my_index, 0, keepdims=False)
    live_f = lax.dynamic_index_in_dim(live_mask, my_index, 0, keepdims=False).astype(jnp.float32)
    grad_sq = slot_grad * slot_grad + EPS_SQUARE
    row_val = DECAY_RATE * row_state[0] + (1.0 - DECAY_RATE) * jnp.mean(grad_sq, axis=1)
    slot_pick = ((my_rows // DKV)[:, None] == jnp.arange(PROJ, dtype=jnp.int32)[None, :]).astype(
        jnp.float32
    )
    live_pick = slot_pick * live_f[:, None]
    col_part = jnp.einsum("sp,sd->pd", live_pick, grad_sq, precision=lax.Precision.HIGHEST)
    row_part = jnp.sum(live_pick * row_val[:, None], axis=0)
    col_sum, row_total = lax.psum((col_part, row_part), "dp")
    new_col = DECAY_RATE * col_state[0] + (1.0 - DECAY_RATE) * col_sum / DKV
    row_mean = row_total / DKV
    col_at = jnp.dot(slot_pick, new_col, precision=lax.Precision.HIGHEST)
    mean_at = jnp.sum(slot_pick * row_mean[None, :], axis=1)
    second_moment = row_val[:, None] * col_at / mean_at[:, None]
    update = slot_grad / jnp.sqrt(second_moment)
    new_param = (
        (param_slots[0].astype(jnp.float32) - STEP_SIZE * update) * live_f[:, None]
    ).astype(jnp.bfloat16)
    return (new_param[None], (row_val * live_f)[None], new_col[None])


EXTRA = 8
COLLECT_FIRST = 6_400_000_000
COLLECT_LAST = 3_000_000_000
MULTIPLY_FIRST = 1_300_000_000
MULTIPLY_LAST = 1_000_000_000
BF16 = jnp.bfloat16
F32 = jnp.float32
VMEM_LIMIT = 16 * 1024 * 1024
BEGIN_LIMIT = 56 * 1024 * 1024


def here_of():
    s = lax.axis_index("shard")
    return lax.axis_index("dp"), s // 2, s % 2


def call(body, out_shape, scratch=(), arrays=0, flops=0, moved=0):
    return pl.pallas_call(
        body,
        out_shape=out_shape,
        in_specs=[pl.BlockSpec(memory_space=pltpu.VMEM)] * arrays,
        out_specs=jax.tree.map(lambda _: pl.BlockSpec(memory_space=pltpu.VMEM), out_shape),
        scratch_shapes=list(scratch),
        compiler_params=pltpu.CompilerParams(vmem_limit_bytes=VMEM_LIMIT),
        cost_estimate=pl.CostEstimate(flops=flops, bytes_accessed=moved, transcendentals=0),
    )


def iota(shape, dim):
    return lax.broadcasted_iota(jnp.int32, shape, dim)


def begin(rows, heads_hbm, owner_hbm, state_hbm, terms_ref, heads_ref, owner_ref, state_ref, sems):
    copies = [
        pltpu.make_async_copy(heads_hbm, heads_ref, sems.at[0]),
        pltpu.make_async_copy(owner_hbm, owner_ref, sems.at[1]),
        pltpu.make_async_copy(state_hbm, state_ref, sems.at[2]),
    ]
    for copy in copies:
        copy.start()
    for copy in copies:
        copy.wait()
    terms_ref[:rows, :] = heads_ref[...].astype(F32).T
    terms_ref[rows : rows + 1, :] = state_ref[...]
    named = owner_ref[...].astype(F32)
    terms_ref[rows + 1 : rows + 2, :] = named[:, : rows // 2]
    terms_ref[rows + 2 : rows + 3, :] = named[:, rows // 2 :]
    terms_ref[rows + 3 :, :] = jnp.zeros((terms_ref.shape[0] - rows - 3, terms_ref.shape[1]), F32)


def columns(inputs_hbm, *refs):
    *outs, inputs_ref, sem = refs
    _, chip, core = here_of()
    half = outs[0].shape[1]
    span = 2 * half
    some = pl.ds(pl.multiple_of(chip * span, 128), span)
    copy = pltpu.make_async_copy(inputs_hbm.at[:, :, some], inputs_ref, sem)
    copy.start()
    copy.wait()
    for c in range(2):
        for side in range(2):
            at = pl.multiple_of((core ^ side) * half, 128)
            outs[2 * c + side][...] = inputs_ref[:, c, pl.ds(at, half)].astype(F32)


def spread(*refs):
    *blocks, out_ref = refs
    at = 0
    for block in blocks:
        value = block[...]
        for j in range(out_ref.shape[0]):
            out_ref[j, :, at : at + value.shape[1]] = value
        at += value.shape[1]


def near_one(up1, down1, out_ref):
    z, _, _ = here_of()
    out_ref[...] = jnp.where(z <= 2, down1[...], up1[...])


def two_away(up2, down2, out_ref):
    z, _, _ = here_of()
    out_ref[...] = jnp.where(z <= 1, down2[...], up2[...])


def last_one(up1, up3, down3, *outs):
    z, _, _ = here_of()
    value = jnp.where(z == 0, down3[...], jnp.where(z == 3, up3[...], up1[...]))
    size = outs[0].shape[0]
    for i, out in enumerate(outs):
        out[...] = value[i * size : (i + 1) * size]


def prepare(heads, rows, pair_most, all_ref, *refs):
    slot_ref, row_ref, last_ref, live_ref, state_ref, total_ref = refs
    z, chip, _ = here_of()
    owners = rows // DKV
    tokens = all_ref.shape[2] // owners
    block = rows // owners
    slots = owners * pair_most
    split, cut = rows - DKV, (owners - 1) * pair_most
    half = rows // 2

    def owner_row(m):
        at = chip ^ m
        return jnp.concatenate(
            [all_ref[at, rows + 1 : rows + 2, :half], all_ref[at, rows + 2 : rows + 3, :half]], axis=1
        )

    lane = iota((rows, rows), 1)
    row = iota((rows, rows), 0)
    earlier = ((row < lane) & (row // block == lane // block)).astype(F32).astype(BF16)
    named = jnp.concatenate(
        [owner_row(m) for m in range(heads)] + [jnp.full((8 - heads, rows), -1.0, F32)], axis=0
    )
    mine = named == z.astype(F32)
    before = jnp.dot(mine.astype(F32).astype(BF16), earlier, preferred_element_type=F32)
    at = iota((8, rows), 1) // block * pair_most
    slot_of = jnp.where(mine, before + at.astype(F32), -1.0)
    slot_id = iota((slots, rows), 0).astype(F32)
    all1 = rows - split + slots - cut
    for m in range(heads):
        terms = all_ref[chip ^ m, :rows, :].astype(BF16)
        pick = (slot_id == slot_of[m : m + 1, :]).astype(F32)
        chosen = jnp.dot(pick.astype(BF16), terms, preferred_element_type=F32).astype(BF16)
        row_ref[m * split : (m + 1) * split, :] = terms[:split]
        slot_ref[m * cut : (m + 1) * cut, :] = chosen[:cut]
        last_ref[m * all1 : m * all1 + rows - split, :] = terms[split:]
        last_ref[m * all1 + rows - split : (m + 1) * all1, :] = chosen[cut:]
        if m == 0:
            live_ref[...] = jnp.sum(pick, axis=1, keepdims=True)
    state = all_ref[chip, rows : rows + 1, :slots]
    same = iota((slots, slots), 0) == iota((slots, slots), 1)
    state_ref[...] = jnp.sum(jnp.where(same, state, 0.0), axis=1, keepdims=True)
    owner_of = jnp.where(
        iota((8, rows), 0) == 0,
        z,
        jnp.where(
            iota((8, rows), 0) == 1,
            (z + owners - 1) % owners,
            jnp.where(iota((8, rows), 0) == 2, (z + 1) % owners, (z + 2) % owners),
        ),
    ).astype(F32)
    theirs = (owner_row(0) == owner_of).astype(F32).astype(BF16)
    home = (iota((rows, slots), 0) // block == iota((rows, slots), 1) // pair_most).astype(F32)
    count = jnp.dot(theirs, home.astype(BF16), preferred_element_type=F32)
    held = (iota((8, slots), 1) % pair_most).astype(F32) < count
    states = [
        all_ref[chip, rows : rows + 1, k * tokens : k * tokens + slots] for k in range(owners)
    ]
    states = jnp.concatenate(states + [jnp.zeros((8 - owners, slots), F32)], axis=0)
    states = jnp.where(held, states, 0.0)
    for i in range(owners):
        part = jnp.where(iota((8, slots), 1) // pair_most == i, states, 0.0)
        part = jnp.sum(jnp.sum(part, axis=1, keepdims=True), axis=0, keepdims=True)
        total_ref[i : i + 1, :] = jnp.broadcast_to(part, (1, slots))


def gather_blocks(held, own, near, got):
    z, _, _ = here_of()
    tokens, half = own.shape
    count = len(got) // 2
    above = jnp.where(z == 3, 1, 2)
    places = (above, 3, 3 - above)
    for side, mine in enumerate((own, near)):
        some = slice(side * half, (side + 1) * half)
        held[:tokens, some] = mine[...].astype(BF16)
        at = 0
        for ref in got[side * count : (side + 1) * count]:
            size = ref.shape[0]
            block, rest = at // tokens, at % tokens
            start = pl.multiple_of(places[block] * tokens + rest, size)
            held[pl.ds(start, size), some] = ref[...].astype(BF16)
            at += size


def multiply(blocks, slot_terms, own, near, *refs):
    got, outs, held = refs[:blocks], refs[blocks:-1], refs[-1]
    gather_blocks(held, own, near, got)
    x = held[...]
    each = outs[0].shape[0]
    for m, out in enumerate(outs):
        out[...] = jnp.dot(
            slot_terms[m * each : (m + 1) * each, :], x, preferred_element_type=F32
        )


def column_sums(heads, row_terms, held, sums_ref):
    x = held[...]
    each = row_terms.shape[0] // heads
    for m in range(heads):
        g = jnp.dot(row_terms[m * each : (m + 1) * each, :], x, preferred_element_type=F32)
        for p in range(PROJ - 1):
            part = g[p * DKV : (p + 1) * DKV]
            sums_ref[m, p : p + 1, :] = jnp.sum(part * part + EPS_SQUARE, axis=0, keepdims=True)


def multiply_last(blocks, slots, terms, own, near, *refs):
    got, sums_ref, outs, held = refs[:blocks], refs[blocks], refs[blocks + 1 : -1], refs[-1]
    gather_blocks(held, own, near, got)
    x = held[...]
    each = DKV + slots
    width = x.shape[1]
    base = width // 128 * slots
    for m, out in enumerate(outs):
        g = jnp.dot(terms[m * each : (m + 1) * each, :], x, preferred_element_type=F32)
        part = g[:DKV]
        last = jnp.sum(part * part + EPS_SQUARE, axis=0, keepdims=True)
        sums = jnp.concatenate([sums_ref[m, : PROJ - 1, :], last], axis=0)
        for j in range(width // 128):
            out[j * slots : (j + 1) * slots, :] = g[DKV:, j * 128 : (j + 1) * 128]
            out[base + j * PROJ : base + (j + 1) * PROJ, :] = sums[:, j * 128 : (j + 1) * 128]


def spans_of(refs, width):
    _, chip, core = here_of()
    heads = len(refs)
    span = width // heads
    half = span // 2
    return [
        (refs[m], side * half, pl.multiple_of((chip ^ m) * span + (core ^ side) * half, 128))
        for m in range(heads)
        for side in range(2)
    ], half


def early(*refs):
    *first, square_ref = refs
    square = jnp.zeros((square_ref.shape[0], 128), F32)
    for ref in first:
        for j in range(0, ref.shape[1], 128):
            g = ref[:, j : j + 128]
            square += g * g + EPS_SQUARE
    square_ref[...] = jnp.sum(square, axis=1, keepdims=True)


def update(heads, pair_most, *refs):
    first, last, refs = refs[:heads], refs[heads : 2 * heads], refs[2 * heads :]
    square0, params, live_ref, state_ref, total_ref, cols, new_params, new_rows, new_cols = refs
    slots, width = params.shape
    rest = pair_most
    span = width // heads
    base = span // 128 * rest
    spans, half = spans_of(first, width)
    spans = [(m, lo, start) for m in range(heads) for _, lo, start in spans[2 * m : 2 * m + 2]]

    def beside(m, lo, offset, count):
        blocks = range(lo // 128, (lo + half) // 128)
        return jnp.concatenate(
            [last[m][offset + j * count : offset + (j + 1) * count, :] for j in blocks], axis=1
        )

    sums = jnp.zeros((PROJ, 128), F32)
    square = jnp.zeros((rest, 128), F32)
    for m, lo, start in spans:
        for j in range(lo // 128, (lo + half) // 128):
            g = last[m][j * rest : (j + 1) * rest, :]
            square += g * g + EPS_SQUARE
            sums += last[m][base + j * PROJ : base + (j + 1) * PROJ, :]
        new_cols[:, pl.ds(start, half)] = (
            DECAY_RATE * cols[:, pl.ds(start, half)]
            + (1.0 - DECAY_RATE) * beside(m, lo, base, PROJ) / DKV
        )
    square = jnp.concatenate([square0[...], jnp.sum(square, axis=1, keepdims=True)], axis=0)
    row_val = DECAY_RATE * state_ref[...] + (1.0 - DECAY_RATE) * (square / width)
    row_mean = (
        DECAY_RATE * total_ref[:, :1]
        + (1.0 - DECAY_RATE) * jnp.sum(sums, axis=1, keepdims=True) / width
    ) / DKV
    mean_at = jnp.concatenate(
        [jnp.broadcast_to(row_mean[i : i + 1], (pair_most, 1)) for i in range(PROJ)], axis=0
    )
    live = live_ref[...]
    row_scale = STEP_SIZE * jnp.sqrt(mean_at / row_val)
    same = iota((slots, slots), 0) == iota((slots, slots), 1)
    new_rows[...] = jnp.sum(jnp.where(same, row_val * live, 0.0), axis=0, keepdims=True)
    for m, lo, start in spans:
        col_scale = lax.rsqrt(new_cols[:, pl.ds(start, half)])
        for i in range(PROJ):
            rows = slice(i * pair_most, (i + 1) * pair_most)
            g = first[m][rows, lo : lo + half] if i < PROJ - 1 else beside(m, lo, 0, rest)
            value = params[rows, pl.ds(start, half)].astype(F32) - g * row_scale[rows] * (
                col_scale[i : i + 1]
            )
            new_params[rows, pl.ds(start, half)] = jnp.where(live[rows] > 0.0, value, 0.0).astype(
                BF16
            )


def gather_step(
    dp_count, shard_count, head_terms, inputs, owner_list, param_slots, row_state, col_state
):
    heads = shard_count // 2
    tokens, _, width = inputs.shape
    rows = head_terms.shape[2]
    slots = param_slots.shape[1]
    pair_most = slots // dp_count
    span = width // heads
    half = span // 2
    split, cut = rows - DKV, slots - pair_most
    depth = dp_count * tokens

    def move(array, dp_to, shard_to=lambda j: j):
        pairs = [
            (i * shard_count + j, dp_to[i] * shard_count + shard_to(j))
            for i in dp_to
            for j in range(shard_count)
        ]
        return lax.ppermute(array, ("dp", "shard"), pairs)

    every = {i: i for i in range(4)}
    upward, downward = {i: i + 1 for i in range(3)}, {i + 1: i for i in range(3)}
    swap = lambda j: j ^ 1

    anywhere = pl.BlockSpec(memory_space=pl.ANY)
    in_vmem = pl.BlockSpec(memory_space=pltpu.VMEM)
    terms = pl.pallas_call(
        functools.partial(begin, rows),
        out_shape=jax.ShapeDtypeStruct((rows + EXTRA, tokens), F32),
        in_specs=[anywhere] * 3,
        out_specs=in_vmem,
        scratch_shapes=[
            pltpu.VMEM((tokens, rows), BF16),
            pltpu.VMEM((1, rows), jnp.int32),
            pltpu.VMEM((1, tokens), F32),
            pltpu.SemaphoreType.DMA((3,)),
        ],
        compiler_params=pltpu.CompilerParams(vmem_limit_bytes=BEGIN_LIMIT),
    )(head_terms[:, 0, :], owner_list[:, :, 0], row_state)
    own0, near0, own1, near1 = pl.pallas_call(
        columns,
        out_shape=[jax.ShapeDtypeStruct((tokens, half), F32)] * 4,
        in_specs=[anywhere],
        out_specs=[in_vmem] * 4,
        scratch_shapes=[pltpu.VMEM((tokens, 2, span), BF16), pltpu.SemaphoreType.DMA(())],
        compiler_params=pltpu.CompilerParams(vmem_limit_bytes=BEGIN_LIMIT),
    )(inputs)

    chips = [[2 * i + c for i in range(heads)] for c in range(2)]
    ring = lambda k: {i: (i + k) % dp_count for i in range(dp_count)}
    def exchange(*blocks):
        size = sum(block.shape[1] for block in blocks)
        everywhere = call(
            spread,
            jax.ShapeDtypeStruct((heads, rows + EXTRA, size), F32),
            arrays=len(blocks),
        )(*blocks)
        return lax.all_to_all(everywhere, "shard", 0, 0, axis_index_groups=chips)

    def chosen(body, parts, cost, *arrays):
        outs = [jax.ShapeDtypeStruct((tokens // parts, half), F32)] * parts
        here = call(body, outs, arrays=len(arrays), flops=cost)(*arrays)
        return here, [move(block, every, swap) for block in here]

    def joined(cost, parts, up1, down1, up2, down2, up3, down3):
        one, one_n = chosen(near_one, 1, 0, up1, down1)
        two, two_n = chosen(two_away, 1, 0, up2, down2)
        three, three_n = chosen(last_one, parts, cost, up1, up3, down3)
        return *one, *two, *three, *one_n, *two_n, *three_n

    def scatter(outs):
        return [
            out if m == 0 else move(out, every, lambda j, m=m: j ^ (2 * m))
            for m, out in enumerate(outs)
        ]

    up1, down1 = move(own0, upward), move(own0, downward)
    ha, hb, hc = [move(terms, ring(k)) for k in (1, dp_count - 1, 2)]
    gathered = exchange(terms, ha, hb, hc)
    up2, down2 = move(up1, upward), move(down1, downward)
    late = lax.optimization_barrier((own1, hc))[0]
    nup1, ndown1 = move(late, upward), move(late, downward)
    up3, down3 = move(up2, upward), move(down2, downward)
    blocks0 = joined(COLLECT_FIRST, 1, up1, down1, up2, down2, up3, down3)
    nup2, ndown2 = move(nup1, upward), move(ndown1, downward)
    slot_terms, row_terms, last_terms, live, state, total = call(
        functools.partial(prepare, heads, rows, pair_most),
        [
            jax.ShapeDtypeStruct((heads * cut, depth), BF16),
            jax.ShapeDtypeStruct((heads * split, depth), BF16),
            jax.ShapeDtypeStruct((heads * (rows - split + slots - cut), depth), BF16),
            jax.ShapeDtypeStruct((slots, 1), F32),
            jax.ShapeDtypeStruct((slots, 1), F32),
            jax.ShapeDtypeStruct((PROJ, slots), F32),
        ],
        arrays=1,
    )(gathered)
    *outs, held0 = call(
        functools.partial(multiply, len(blocks0)),
        [jax.ShapeDtypeStruct((cut, span), F32)] * heads + [jax.ShapeDtypeStruct((depth, span), BF16)],
        arrays=3 + len(blocks0),
        flops=MULTIPLY_FIRST,
    )(slot_terms, own0, near0, *blocks0)
    sums0 = call(
        functools.partial(column_sums, heads),
        jax.ShapeDtypeStruct((heads, 8, span), F32),
        arrays=2,
    )(row_terms, held0)
    first = scatter(outs)
    nup3, ndown3 = move(nup2, upward), move(ndown2, downward)
    blocks1 = joined(COLLECT_LAST, 2, nup1, ndown1, nup2, ndown2, nup3, ndown3)
    rest = slots - cut
    last = scatter(
        call(
            functools.partial(multiply_last, len(blocks1), rest),
            [jax.ShapeDtypeStruct((span // 128 * (rest + PROJ), 128), F32)] * heads,
            scratch=[pltpu.VMEM((depth, span), BF16)],
            arrays=4 + len(blocks1),
            flops=MULTIPLY_LAST,
        )(last_terms, own1, near1, *blocks1, sums0)
    )
    square0 = call(
        early,
        jax.ShapeDtypeStruct((cut, 1), F32),
        arrays=heads,
    )(*first)
    new_params, new_rows, new_cols = call(
        functools.partial(update, heads, pair_most),
        [
            jax.ShapeDtypeStruct((slots, width), BF16),
            jax.ShapeDtypeStruct((1, slots), F32),
            jax.ShapeDtypeStruct((PROJ, width), F32),
        ],
        arrays=2 * heads + 6,
        moved=4 * slots * width * 2,
    )(*first, *last, square0, param_slots[0], live, state, total, col_state[0])
    return (new_params[None], new_rows, new_cols[None])


def one_step(mesh, *args):
    dp_count, shard_count = mesh.shape["dp"], mesh.shape["shard"]
    tokens, slots, rows = args[1].shape[0], args[3].shape[1], args[0].shape[2]
    if dp_count == 4 and shard_count == 8 and tokens == slots and rows == PROJ * DKV:
        return gather_step(dp_count, shard_count, *args)
    return general_step(*args)


def solution(mesh):
    placed = (
        P("dp", "shard", None),
        P("dp", None, None),
        P("shard", None, None),
        P("shard", "dp", None),
        P("shard", "dp"),
        P("shard", None, None),
    )
    return jax.shard_map(
        functools.partial(one_step, mesh),
        mesh=mesh,
        in_specs=placed,
        out_specs=(P("shard", "dp", None), P("shard", "dp"), P("shard", None, None)),
        check_vma=False,
    )
```

```python
import functools

import jax
import jax.numpy as jnp
from jax import lax
from jax.experimental import pallas as pl
from jax.experimental.pallas import tpu as pltpu
from jax.sharding import PartitionSpec as P

DKV = 64
PROJ = 4


DECAY_RATE = 0.5
STEP_SIZE = 0.5
EPS_SQUARE = 1e-30


def slot_table(owner_col, owner_count, pair_most):
    row_count = owner_col.shape[0]
    block_rows = row_count // owner_count
    index_ids = jnp.arange(owner_count, dtype=jnp.int32)
    onehot = (owner_col[:, None] == index_ids[None, :]).astype(jnp.int32)
    blocked = onehot.reshape(owner_count, block_rows, owner_count)
    before = jnp.cumsum(blocked, axis=1) - blocked
    order_in = jnp.sum(before * blocked, axis=2).reshape(row_count)
    row_ids = jnp.arange(row_count, dtype=jnp.int32)
    block_of = row_ids // block_rows
    slot_ids = jnp.arange(pair_most, dtype=jnp.int32)
    match_owner = owner_col[None, None, None, :] == index_ids[:, None, None, None]
    match_block = block_of[None, None, None, :] == index_ids[None, :, None, None]
    match_slot = order_in[None, None, None, :] == slot_ids[None, None, :, None]
    hits = (match_owner & match_block & match_slot).astype(jnp.int32)
    live_mask = jnp.sum(hits, axis=3).reshape(owner_count, owner_count * pair_most)
    slot_row = jnp.sum(hits * row_ids[None, None, None, :], axis=3).reshape(
        owner_count, owner_count * pair_most
    )
    return (slot_row, live_mask)


def general_step(head_terms, inputs, owner_list, param_slots, row_state, col_state):
    dp_count = lax.axis_size("dp")
    my_index = lax.axis_index("dp")
    head_rows = head_terms[:, 0, :]
    row_count = head_rows.shape[1]
    width = inputs.shape[2]
    slot_count = param_slots.shape[1]
    pair_most = slot_count // dp_count
    block_rows = row_count // dp_count
    split_at = (PROJ - 1) * DKV
    first_part = jnp.einsum(
        "tr,td->rd", head_rows[:, :split_at], inputs[:, 0, :], preferred_element_type=jnp.float32
    )
    last_part = jnp.einsum(
        "tr,td->rd", head_rows[:, split_at:], inputs[:, 1, :], preferred_element_type=jnp.float32
    )
    gradient = jnp.concatenate([first_part, last_part], axis=0)
    slot_row, live_mask = slot_table(owner_list[0, :, 0], dp_count, pair_most)
    home_sum = lax.psum_scatter(gradient, "dp", scatter_dimension=0, tiled=True)
    local_rows = (
        lax.dynamic_slice_in_dim(slot_row, my_index * pair_most, pair_most, 1)
        - my_index * block_rows
    )
    outgoing = jnp.take(home_sum, local_rows.reshape(-1), axis=0, mode="clip").reshape(
        dp_count, pair_most, width
    )
    received = lax.all_to_all(outgoing, "dp", split_axis=0, concat_axis=0, tiled=True)
    slot_grad = received.reshape(slot_count, width)
    my_rows = lax.dynamic_index_in_dim(slot_row, my_index, 0, keepdims=False)
    live_f = lax.dynamic_index_in_dim(live_mask, my_index, 0, keepdims=False).astype(jnp.float32)
    grad_sq = slot_grad * slot_grad + EPS_SQUARE
    row_val = DECAY_RATE * row_state[0] + (1.0 - DECAY_RATE) * jnp.mean(grad_sq, axis=1)
    slot_pick = ((my_rows // DKV)[:, None] == jnp.arange(PROJ, dtype=jnp.int32)[None, :]).astype(
        jnp.float32
    )
    live_pick = slot_pick * live_f[:, None]
    col_part = jnp.einsum("sp,sd->pd", live_pick, grad_sq, precision=lax.Precision.HIGHEST)
    row_part = jnp.sum(live_pick * row_val[:, None], axis=0)
    col_sum, row_total = lax.psum((col_part, row_part), "dp")
    new_col = DECAY_RATE * col_state[0] + (1.0 - DECAY_RATE) * col_sum / DKV
    row_mean = row_total / DKV
    col_at = jnp.dot(slot_pick, new_col, precision=lax.Precision.HIGHEST)
    mean_at = jnp.sum(slot_pick * row_mean[None, :], axis=1)
    second_moment = row_val[:, None] * col_at / mean_at[:, None]
    update = slot_grad / jnp.sqrt(second_moment)
    new_param = (
        (param_slots[0].astype(jnp.float32) - STEP_SIZE * update) * live_f[:, None]
    ).astype(jnp.bfloat16)
    return (new_param[None], (row_val * live_f)[None], new_col[None])


EXTRA = 8
COLLECT_FIRST = 6_400_000_000
COLLECT_LAST = 3_000_000_000
NEAR_FIRST = 1_000_000_000
NEAR_LAST = 0
MULTIPLY_FIRST = 1_300_000_000
MULTIPLY_LAST = 1_000_000_000
BF16 = jnp.bfloat16
F32 = jnp.float32
VMEM_LIMIT = 16 * 1024 * 1024
BEGIN_LIMIT = 56 * 1024 * 1024


def here_of():
    s = lax.axis_index("shard")
    return lax.axis_index("dp"), s // 2, s % 2


def call(body, out_shape, scratch=(), arrays=0, flops=0, moved=0):
    return pl.pallas_call(
        body,
        out_shape=out_shape,
        in_specs=[pl.BlockSpec(memory_space=pltpu.VMEM)] * arrays,
        out_specs=jax.tree.map(lambda _: pl.BlockSpec(memory_space=pltpu.VMEM), out_shape),
        scratch_shapes=list(scratch),
        compiler_params=pltpu.CompilerParams(vmem_limit_bytes=VMEM_LIMIT),
        cost_estimate=pl.CostEstimate(flops=flops, bytes_accessed=moved, transcendentals=0),
    )


def iota(shape, dim):
    return lax.broadcasted_iota(jnp.int32, shape, dim)


def begin(rows, heads_hbm, owner_hbm, state_hbm, terms_ref, heads_ref, owner_ref, state_ref, sems):
    copies = [
        pltpu.make_async_copy(heads_hbm, heads_ref, sems.at[0]),
        pltpu.make_async_copy(owner_hbm, owner_ref, sems.at[1]),
        pltpu.make_async_copy(state_hbm, state_ref, sems.at[2]),
    ]
    for copy in copies:
        copy.start()
    for copy in copies:
        copy.wait()
    terms_ref[:rows, :] = heads_ref[...].astype(F32).T
    terms_ref[rows : rows + 1, :] = state_ref[...]
    named = owner_ref[...].astype(F32)
    terms_ref[rows + 1 : rows + 2, :] = named[:, : rows // 2]
    terms_ref[rows + 2 : rows + 3, :] = named[:, rows // 2 :]
    terms_ref[rows + 3 :, :] = jnp.zeros((terms_ref.shape[0] - rows - 3, terms_ref.shape[1]), F32)


def columns(inputs_hbm, *refs):
    *outs, inputs_ref, sem = refs
    _, chip, core = here_of()
    half = outs[0].shape[1]
    span = 2 * half
    some = pl.ds(pl.multiple_of(chip * span, 128), span)
    copy = pltpu.make_async_copy(inputs_hbm.at[:, :, some], inputs_ref, sem)
    copy.start()
    copy.wait()
    for c in range(2):
        for side in range(2):
            at = pl.multiple_of((core ^ side) * half, 128)
            outs[2 * c + side][...] = inputs_ref[:, c, pl.ds(at, half)].astype(F32)


def spread(*refs):
    *blocks, out_ref = refs
    at = 0
    for block in blocks:
        value = block[...]
        for j in range(out_ref.shape[0]):
            out_ref[j, :, at : at + value.shape[1]] = value
        at += value.shape[1]


def near_one(up1, down1, out_ref):
    z, _, _ = here_of()
    out_ref[...] = jnp.where(z <= 2, down1[...], up1[...])


def two_away(up2, down2, out_ref):
    z, _, _ = here_of()
    out_ref[...] = jnp.where(z <= 1, down2[...], up2[...])


def last_one(up1, up3, down3, *outs):
    z, _, _ = here_of()
    value = jnp.where(z == 0, down3[...], jnp.where(z == 3, up3[...], up1[...]))
    size = outs[0].shape[0]
    for i, out in enumerate(outs):
        out[...] = value[i * size : (i + 1) * size]


def prepare(heads, rows, pair_most, all_ref, *refs):
    slot_ref, row_ref, last_ref, live_ref, state_ref, total_ref = refs
    z, chip, _ = here_of()
    owners = rows // DKV
    tokens = all_ref.shape[2] // owners
    block = rows // owners
    slots = owners * pair_most
    split, cut = rows - DKV, (owners - 1) * pair_most
    half = rows // 2

    def owner_row(m):
        at = chip ^ m
        return jnp.concatenate(
            [all_ref[at, rows + 1 : rows + 2, :half], all_ref[at, rows + 2 : rows + 3, :half]], axis=1
        )

    lane = iota((rows, rows), 1)
    row = iota((rows, rows), 0)
    earlier = ((row < lane) & (row // block == lane // block)).astype(F32).astype(BF16)
    named = jnp.concatenate(
        [owner_row(m) for m in range(heads)] + [jnp.full((8 - heads, rows), -1.0, F32)], axis=0
    )
    mine = named == z.astype(F32)
    before = jnp.dot(mine.astype(F32).astype(BF16), earlier, preferred_element_type=F32)
    at = iota((8, rows), 1) // block * pair_most
    slot_of = jnp.where(mine, before + at.astype(F32), -1.0)
    slot_id = iota((slots, rows), 0).astype(F32)
    all1 = rows - split + slots - cut
    for m in range(heads):
        terms = all_ref[chip ^ m, :rows, :].astype(BF16)
        pick = (slot_id == slot_of[m : m + 1, :]).astype(F32)
        chosen = jnp.dot(pick.astype(BF16), terms, preferred_element_type=F32).astype(BF16)
        row_ref[m * split : (m + 1) * split, :] = terms[:split]
        slot_ref[m * cut : (m + 1) * cut, :] = chosen[:cut]
        last_ref[m * all1 : m * all1 + rows - split, :] = terms[split:]
        last_ref[m * all1 + rows - split : (m + 1) * all1, :] = chosen[cut:]
        if m == 0:
            live_ref[...] = jnp.sum(pick, axis=1, keepdims=True)
    state = all_ref[chip, rows : rows + 1, :slots]
    same = iota((slots, slots), 0) == iota((slots, slots), 1)
    state_ref[...] = jnp.sum(jnp.where(same, state, 0.0), axis=1, keepdims=True)
    owner_of = jnp.where(
        iota((8, rows), 0) == 0,
        z,
        jnp.where(
            iota((8, rows), 0) == 1,
            (z + owners - 1) % owners,
            jnp.where(iota((8, rows), 0) == 2, (z + 1) % owners, (z + 2) % owners),
        ),
    ).astype(F32)
    theirs = (owner_row(0) == owner_of).astype(F32).astype(BF16)
    home = (iota((rows, slots), 0) // block == iota((rows, slots), 1) // pair_most).astype(F32)
    count = jnp.dot(theirs, home.astype(BF16), preferred_element_type=F32)
    held = (iota((8, slots), 1) % pair_most).astype(F32) < count
    states = [
        all_ref[chip, rows : rows + 1, k * tokens : k * tokens + slots] for k in range(owners)
    ]
    states = jnp.concatenate(states + [jnp.zeros((8 - owners, slots), F32)], axis=0)
    states = jnp.where(held, states, 0.0)
    for i in range(owners):
        part = jnp.where(iota((8, slots), 1) // pair_most == i, states, 0.0)
        part = jnp.sum(jnp.sum(part, axis=1, keepdims=True), axis=0, keepdims=True)
        total_ref[i : i + 1, :] = jnp.broadcast_to(part, (1, slots))


def gather_blocks(held, own, near, got):
    z, _, _ = here_of()
    tokens, half = own.shape
    count = len(got) // 2
    above = jnp.where(z == 3, 1, 2)
    places = (above, 3, 3 - above)
    for side, mine in enumerate((own, near)):
        some = slice(side * half, (side + 1) * half)
        held[:tokens, some] = mine[...].astype(BF16)
        at = 0
        for ref in got[side * count : (side + 1) * count]:
            size = ref.shape[0]
            block, rest = at // tokens, at % tokens
            start = pl.multiple_of(places[block] * tokens + rest, size)
            held[pl.ds(start, size), some] = ref[...].astype(BF16)
            at += size


def multiply(blocks, slot_terms, own, near, *refs):
    got, outs, held = refs[:blocks], refs[blocks:-1], refs[-1]
    gather_blocks(held, own, near, got)
    x = held[...]
    each = outs[0].shape[0]
    g = jnp.dot(slot_terms[...], x, preferred_element_type=F32)
    for m, out in enumerate(outs):
        out[...] = g[m * each : (m + 1) * each]


def column_sums(heads, row_terms, held, sums_ref):
    x = held[...]
    each = row_terms.shape[0] // heads
    every = jnp.dot(row_terms[...], x, preferred_element_type=F32)
    for m in range(heads):
        for p in range(PROJ - 1):
            part = every[m * each + p * DKV : m * each + (p + 1) * DKV]
            sums_ref[m, p : p + 1, :] = jnp.sum(part * part + EPS_SQUARE, axis=0, keepdims=True)


def multiply_last(blocks, slots, terms, own, near, *refs):
    got, sums_ref, outs, held = refs[:blocks], refs[blocks], refs[blocks + 1 : -1], refs[-1]
    gather_blocks(held, own, near, got)
    x = held[...]
    each = DKV + slots
    width = x.shape[1]
    base = width // 128 * slots
    every = jnp.dot(terms[...], x, preferred_element_type=F32)
    for m, out in enumerate(outs):
        g = every[m * each : (m + 1) * each]
        part = g[:DKV]
        last = jnp.sum(part * part + EPS_SQUARE, axis=0, keepdims=True)
        sums = jnp.concatenate([sums_ref[m, : PROJ - 1, :], last], axis=0)
        for j in range(width // 128):
            out[j * slots : (j + 1) * slots, :] = g[DKV:, j * 128 : (j + 1) * 128]
            out[base + j * PROJ : base + (j + 1) * PROJ, :] = sums[:, j * 128 : (j + 1) * 128]


def spans_of(refs, width):
    _, chip, core = here_of()
    heads = len(refs)
    span = width // heads
    half = span // 2
    return [
        (refs[m], side * half, pl.multiple_of((chip ^ m) * span + (core ^ side) * half, 128))
        for m in range(heads)
        for side in range(2)
    ], half


def early(*refs):
    *first, square_ref = refs
    square = jnp.zeros((square_ref.shape[0], 128), F32)
    for ref in first:
        for j in range(0, ref.shape[1], 128):
            g = ref[:, j : j + 128]
            square += g * g + EPS_SQUARE
    square_ref[...] = jnp.sum(square, axis=1, keepdims=True)


def update(heads, pair_most, *refs):
    first, last, refs = refs[:heads], refs[heads : 2 * heads], refs[2 * heads :]
    square0, params, live_ref, state_ref, total_ref, cols, new_params, new_rows, new_cols = refs
    slots, width = params.shape
    rest = pair_most
    span = width // heads
    base = span // 128 * rest
    spans, half = spans_of(first, width)
    spans = [(m, lo, start) for m in range(heads) for _, lo, start in spans[2 * m : 2 * m + 2]]

    def beside(m, lo, offset, count):
        blocks = range(lo // 128, (lo + half) // 128)
        return jnp.concatenate(
            [last[m][offset + j * count : offset + (j + 1) * count, :] for j in blocks], axis=1
        )

    sums = jnp.zeros((PROJ, 128), F32)
    square = jnp.zeros((rest, 128), F32)
    for m, lo, start in spans:
        for j in range(lo // 128, (lo + half) // 128):
            g = last[m][j * rest : (j + 1) * rest, :]
            square += g * g + EPS_SQUARE
            sums += last[m][base + j * PROJ : base + (j + 1) * PROJ, :]
        new_cols[:, pl.ds(start, half)] = (
            DECAY_RATE * cols[:, pl.ds(start, half)]
            + (1.0 - DECAY_RATE) * beside(m, lo, base, PROJ) / DKV
        )
    square = jnp.concatenate([square0[...], jnp.sum(square, axis=1, keepdims=True)], axis=0)
    row_val = DECAY_RATE * state_ref[...] + (1.0 - DECAY_RATE) * (square / width)
    row_mean = (
        DECAY_RATE * total_ref[:, :1]
        + (1.0 - DECAY_RATE) * jnp.sum(sums, axis=1, keepdims=True) / width
    ) / DKV
    mean_at = jnp.concatenate(
        [jnp.broadcast_to(row_mean[i : i + 1], (pair_most, 1)) for i in range(PROJ)], axis=0
    )
    live = live_ref[...]
    row_scale = STEP_SIZE * jnp.sqrt(mean_at / row_val)
    same = iota((slots, slots), 0) == iota((slots, slots), 1)
    new_rows[...] = jnp.sum(jnp.where(same, row_val * live, 0.0), axis=0, keepdims=True)
    for m, lo, start in spans:
        col_scale = lax.rsqrt(new_cols[:, pl.ds(start, half)])
        for i in range(PROJ):
            rows = slice(i * pair_most, (i + 1) * pair_most)
            g = first[m][rows, lo : lo + half] if i < PROJ - 1 else beside(m, lo, 0, rest)
            value = params[rows, pl.ds(start, half)].astype(F32) - g * row_scale[rows] * (
                col_scale[i : i + 1]
            )
            new_params[rows, pl.ds(start, half)] = jnp.where(live[rows] > 0.0, value, 0.0).astype(
                BF16
            )


def gather_step(
    dp_count, shard_count, head_terms, inputs, owner_list, param_slots, row_state, col_state
):
    heads = shard_count // 2
    tokens, _, width = inputs.shape
    rows = head_terms.shape[2]
    slots = param_slots.shape[1]
    pair_most = slots // dp_count
    span = width // heads
    half = span // 2
    split, cut = rows - DKV, slots - pair_most
    depth = dp_count * tokens

    def move(array, dp_to, shard_to=lambda j: j):
        pairs = [
            (i * shard_count + j, dp_to[i] * shard_count + shard_to(j))
            for i in dp_to
            for j in range(shard_count)
        ]
        return lax.ppermute(array, ("dp", "shard"), pairs)

    every = {i: i for i in range(4)}
    upward, downward = {i: i + 1 for i in range(3)}, {i + 1: i for i in range(3)}
    swap = lambda j: j ^ 1

    anywhere = pl.BlockSpec(memory_space=pl.ANY)
    in_vmem = pl.BlockSpec(memory_space=pltpu.VMEM)
    terms = pl.pallas_call(
        functools.partial(begin, rows),
        out_shape=jax.ShapeDtypeStruct((rows + EXTRA, tokens), F32),
        in_specs=[anywhere] * 3,
        out_specs=in_vmem,
        scratch_shapes=[
            pltpu.VMEM((tokens, rows), BF16),
            pltpu.VMEM((1, rows), jnp.int32),
            pltpu.VMEM((1, tokens), F32),
            pltpu.SemaphoreType.DMA((3,)),
        ],
        compiler_params=pltpu.CompilerParams(vmem_limit_bytes=BEGIN_LIMIT),
    )(head_terms[:, 0, :], owner_list[:, :, 0], row_state)
    own0, near0, own1, near1 = pl.pallas_call(
        columns,
        out_shape=[jax.ShapeDtypeStruct((tokens, half), F32)] * 4,
        in_specs=[anywhere],
        out_specs=[in_vmem] * 4,
        scratch_shapes=[pltpu.VMEM((tokens, 2, span), BF16), pltpu.SemaphoreType.DMA(())],
        compiler_params=pltpu.CompilerParams(vmem_limit_bytes=BEGIN_LIMIT),
    )(inputs)

    chips = [[2 * i + c for i in range(heads)] for c in range(2)]
    ring = lambda k: {i: (i + k) % dp_count for i in range(dp_count)}
    def exchange(*blocks):
        size = sum(block.shape[1] for block in blocks)
        everywhere = call(
            spread,
            jax.ShapeDtypeStruct((heads, rows + EXTRA, size), F32),
            arrays=len(blocks),
        )(*blocks)
        return lax.all_to_all(everywhere, "shard", 0, 0, axis_index_groups=chips)

    def chosen(body, parts, cost, *arrays):
        outs = [jax.ShapeDtypeStruct((tokens // parts, half), F32)] * parts
        here = call(body, outs, arrays=len(arrays), flops=cost)(*arrays)
        return here, [move(block, every, swap) for block in here]

    def joined(cost, before, parts, up1, down1, up2, down2, up3, down3):
        one, one_n = chosen(near_one, 1, before, up1, down1)
        two, two_n = chosen(two_away, 1, before, up2, down2)
        three, three_n = chosen(last_one, parts, cost, up1, up3, down3)
        return *one, *two, *three, *one_n, *two_n, *three_n

    def scatter(outs):
        return [
            out if m == 0 else move(out, every, lambda j, m=m: j ^ (2 * m))
            for m, out in enumerate(outs)
        ]

    up1, down1 = move(own0, upward), move(own0, downward)
    ha, hb, hc = [move(terms, ring(k)) for k in (1, dp_count - 1, 2)]
    gathered = exchange(terms, ha, hb, hc)
    up2, down2 = move(up1, upward), move(down1, downward)
    late = lax.optimization_barrier((own1, hc))[0]
    nup1, ndown1 = move(late, upward), move(late, downward)
    up3, down3 = move(up2, upward), move(down2, downward)
    blocks0 = joined(COLLECT_FIRST, NEAR_FIRST, 1, up1, down1, up2, down2, up3, down3)
    nup2, ndown2 = move(nup1, upward), move(ndown1, downward)
    slot_terms, row_terms, last_terms, live, state, total = call(
        functools.partial(prepare, heads, rows, pair_most),
        [
            jax.ShapeDtypeStruct((heads * cut, depth), BF16),
            jax.ShapeDtypeStruct((heads * split, depth), BF16),
            jax.ShapeDtypeStruct((heads * (rows - split + slots - cut), depth), BF16),
            jax.ShapeDtypeStruct((slots, 1), F32),
            jax.ShapeDtypeStruct((slots, 1), F32),
            jax.ShapeDtypeStruct((PROJ, slots), F32),
        ],
        arrays=1,
    )(gathered)
    *outs, held0 = call(
        functools.partial(multiply, len(blocks0)),
        [jax.ShapeDtypeStruct((cut, span), F32)] * heads + [jax.ShapeDtypeStruct((depth, span), BF16)],
        arrays=3 + len(blocks0),
        flops=MULTIPLY_FIRST,
    )(slot_terms, own0, near0, *blocks0)
    sums0 = call(
        functools.partial(column_sums, heads),
        jax.ShapeDtypeStruct((heads, 8, span), F32),
        arrays=2,
    )(row_terms, held0)
    first = scatter(outs)
    nup3, ndown3 = move(nup2, upward), move(ndown2, downward)
    blocks1 = joined(COLLECT_LAST, NEAR_LAST, 2, nup1, ndown1, nup2, ndown2, nup3, ndown3)
    rest = slots - cut
    last = scatter(
        call(
            functools.partial(multiply_last, len(blocks1), rest),
            [jax.ShapeDtypeStruct((span // 128 * (rest + PROJ), 128), F32)] * heads,
            scratch=[pltpu.VMEM((depth, span), BF16)],
            arrays=4 + len(blocks1),
            flops=MULTIPLY_LAST,
        )(last_terms, own1, near1, *blocks1, sums0)
    )
    square0 = call(
        early,
        jax.ShapeDtypeStruct((cut, 1), F32),
        arrays=heads,
    )(*first)
    new_params, new_rows, new_cols = call(
        functools.partial(update, heads, pair_most),
        [
            jax.ShapeDtypeStruct((slots, width), BF16),
            jax.ShapeDtypeStruct((1, slots), F32),
            jax.ShapeDtypeStruct((PROJ, width), F32),
        ],
        arrays=2 * heads + 6,
        moved=4 * slots * width * 2,
    )(*first, *last, square0, param_slots[0], live, state, total, col_state[0])
    return (new_params[None], new_rows, new_cols[None])


def one_step(mesh, *args):
    dp_count, shard_count = mesh.shape["dp"], mesh.shape["shard"]
    tokens, slots, rows = args[1].shape[0], args[3].shape[1], args[0].shape[2]
    if dp_count == 4 and shard_count == 8 and tokens == slots and rows == PROJ * DKV:
        return gather_step(dp_count, shard_count, *args)
    return general_step(*args)


def solution(mesh):
    placed = (
        P("dp", "shard", None),
        P("dp", None, None),
        P("shard", None, None),
        P("shard", "dp", None),
        P("shard", "dp"),
        P("shard", None, None),
    )
    return jax.shard_map(
        functools.partial(one_step, mesh),
        mesh=mesh,
        in_specs=placed,
        out_specs=(P("shard", "dp", None), P("shard", "dp"), P("shard", None, None)),
        check_vma=False,
    )
```

```python
import functools

import jax
import jax.numpy as jnp
from jax import lax
from jax.experimental import pallas as pl
from jax.experimental.pallas import tpu as pltpu
from jax.sharding import PartitionSpec as P

DKV = 64
PROJ = 4


DECAY_RATE = 0.5
STEP_SIZE = 0.5
EPS_SQUARE = 1e-30


def slot_table(owner_col, owner_count, pair_most):
    row_count = owner_col.shape[0]
    block_rows = row_count // owner_count
    index_ids = jnp.arange(owner_count, dtype=jnp.int32)
    onehot = (owner_col[:, None] == index_ids[None, :]).astype(jnp.int32)
    blocked = onehot.reshape(owner_count, block_rows, owner_count)
    before = jnp.cumsum(blocked, axis=1) - blocked
    order_in = jnp.sum(before * blocked, axis=2).reshape(row_count)
    row_ids = jnp.arange(row_count, dtype=jnp.int32)
    block_of = row_ids // block_rows
    slot_ids = jnp.arange(pair_most, dtype=jnp.int32)
    match_owner = owner_col[None, None, None, :] == index_ids[:, None, None, None]
    match_block = block_of[None, None, None, :] == index_ids[None, :, None, None]
    match_slot = order_in[None, None, None, :] == slot_ids[None, None, :, None]
    hits = (match_owner & match_block & match_slot).astype(jnp.int32)
    live_mask = jnp.sum(hits, axis=3).reshape(owner_count, owner_count * pair_most)
    slot_row = jnp.sum(hits * row_ids[None, None, None, :], axis=3).reshape(
        owner_count, owner_count * pair_most
    )
    return (slot_row, live_mask)


def general_step(head_terms, inputs, owner_list, param_slots, row_state, col_state):
    dp_count = lax.axis_size("dp")
    my_index = lax.axis_index("dp")
    head_rows = head_terms[:, 0, :]
    row_count = head_rows.shape[1]
    width = inputs.shape[2]
    slot_count = param_slots.shape[1]
    pair_most = slot_count // dp_count
    block_rows = row_count // dp_count
    split_at = (PROJ - 1) * DKV
    first_part = jnp.einsum(
        "tr,td->rd", head_rows[:, :split_at], inputs[:, 0, :], preferred_element_type=jnp.float32
    )
    last_part = jnp.einsum(
        "tr,td->rd", head_rows[:, split_at:], inputs[:, 1, :], preferred_element_type=jnp.float32
    )
    gradient = jnp.concatenate([first_part, last_part], axis=0)
    slot_row, live_mask = slot_table(owner_list[0, :, 0], dp_count, pair_most)
    home_sum = lax.psum_scatter(gradient, "dp", scatter_dimension=0, tiled=True)
    local_rows = (
        lax.dynamic_slice_in_dim(slot_row, my_index * pair_most, pair_most, 1)
        - my_index * block_rows
    )
    outgoing = jnp.take(home_sum, local_rows.reshape(-1), axis=0, mode="clip").reshape(
        dp_count, pair_most, width
    )
    received = lax.all_to_all(outgoing, "dp", split_axis=0, concat_axis=0, tiled=True)
    slot_grad = received.reshape(slot_count, width)
    my_rows = lax.dynamic_index_in_dim(slot_row, my_index, 0, keepdims=False)
    live_f = lax.dynamic_index_in_dim(live_mask, my_index, 0, keepdims=False).astype(jnp.float32)
    grad_sq = slot_grad * slot_grad + EPS_SQUARE
    row_val = DECAY_RATE * row_state[0] + (1.0 - DECAY_RATE) * jnp.mean(grad_sq, axis=1)
    slot_pick = ((my_rows // DKV)[:, None] == jnp.arange(PROJ, dtype=jnp.int32)[None, :]).astype(
        jnp.float32
    )
    live_pick = slot_pick * live_f[:, None]
    col_part = jnp.einsum("sp,sd->pd", live_pick, grad_sq, precision=lax.Precision.HIGHEST)
    row_part = jnp.sum(live_pick * row_val[:, None], axis=0)
    col_sum, row_total = lax.psum((col_part, row_part), "dp")
    new_col = DECAY_RATE * col_state[0] + (1.0 - DECAY_RATE) * col_sum / DKV
    row_mean = row_total / DKV
    col_at = jnp.dot(slot_pick, new_col, precision=lax.Precision.HIGHEST)
    mean_at = jnp.sum(slot_pick * row_mean[None, :], axis=1)
    second_moment = row_val[:, None] * col_at / mean_at[:, None]
    update = slot_grad / jnp.sqrt(second_moment)
    new_param = (
        (param_slots[0].astype(jnp.float32) - STEP_SIZE * update) * live_f[:, None]
    ).astype(jnp.bfloat16)
    return (new_param[None], (row_val * live_f)[None], new_col[None])


EXTRA = 8
COLLECT_FIRST = 6_400_000_000
COLLECT_LAST = 3_000_000_000
NEAR_FIRST = 1_000_000_000
NEAR_LAST = 0
MULTIPLY_FIRST = 1_300_000_000
MULTIPLY_LAST = 1_000_000_000
BF16 = jnp.bfloat16
F32 = jnp.float32
VMEM_LIMIT = 16 * 1024 * 1024
BEGIN_LIMIT = 56 * 1024 * 1024


def here_of():
    s = lax.axis_index("shard")
    return lax.axis_index("dp"), s // 2, s % 2


def call(body, out_shape, scratch=(), arrays=0, flops=0, moved=0):
    return pl.pallas_call(
        body,
        out_shape=out_shape,
        in_specs=[pl.BlockSpec(memory_space=pltpu.VMEM)] * arrays,
        out_specs=jax.tree.map(lambda _: pl.BlockSpec(memory_space=pltpu.VMEM), out_shape),
        scratch_shapes=list(scratch),
        compiler_params=pltpu.CompilerParams(vmem_limit_bytes=VMEM_LIMIT),
        cost_estimate=pl.CostEstimate(flops=flops, bytes_accessed=moved, transcendentals=0),
    )


def iota(shape, dim):
    return lax.broadcasted_iota(jnp.int32, shape, dim)


def begin(rows, heads_hbm, owner_hbm, state_hbm, terms_ref, heads_ref, owner_ref, state_ref, sems):
    copies = [
        pltpu.make_async_copy(heads_hbm, heads_ref, sems.at[0]),
        pltpu.make_async_copy(owner_hbm, owner_ref, sems.at[1]),
        pltpu.make_async_copy(state_hbm, state_ref, sems.at[2]),
    ]
    for copy in copies:
        copy.start()
    for copy in copies:
        copy.wait()
    terms_ref[:rows, :] = heads_ref[...].astype(F32).T
    terms_ref[rows : rows + 1, :] = state_ref[...]
    named = owner_ref[...].astype(F32)
    terms_ref[rows + 1 : rows + 2, :] = named[:, : rows // 2]
    terms_ref[rows + 2 : rows + 3, :] = named[:, rows // 2 :]
    terms_ref[rows + 3 :, :] = jnp.zeros((terms_ref.shape[0] - rows - 3, terms_ref.shape[1]), F32)


def columns(inputs_hbm, *refs):
    *outs, inputs_ref, sem = refs
    _, chip, core = here_of()
    half = outs[0].shape[1]
    span = 2 * half
    some = pl.ds(pl.multiple_of(chip * span, 128), span)
    copy = pltpu.make_async_copy(inputs_hbm.at[:, :, some], inputs_ref, sem)
    copy.start()
    copy.wait()
    for c in range(2):
        for side in range(2):
            at = pl.multiple_of((core ^ side) * half, 128)
            out = outs[2 * c + side]
            out[...] = inputs_ref[:, c, pl.ds(at, half)].astype(F32).astype(out.dtype)


def spread(*refs):
    *blocks, out_ref = refs
    at = 0
    for block in blocks:
        value = block[...]
        for j in range(out_ref.shape[0]):
            out_ref[j, :, at : at + value.shape[1]] = value
        at += value.shape[1]


def near_one(up1, down1, out_ref):
    z, _, _ = here_of()
    out_ref[...] = jnp.where(z <= 2, down1[...], up1[...])


def two_away(up2, down2, out_ref):
    z, _, _ = here_of()
    out_ref[...] = jnp.where(z <= 1, down2[...], up2[...])


def last_one(up1, up3, down3, *outs):
    z, _, _ = here_of()
    value = jnp.where(z == 0, down3[...], jnp.where(z == 3, up3[...], up1[...]))
    size = outs[0].shape[0]
    for i, out in enumerate(outs):
        out[...] = value[i * size : (i + 1) * size]


def prepare(heads, rows, pair_most, all_ref, *refs):
    slot_ref, row_ref, last_ref, live_ref, state_ref, total_ref = refs
    z, chip, _ = here_of()
    owners = rows // DKV
    tokens = all_ref.shape[2] // owners
    block = rows // owners
    slots = owners * pair_most
    split, cut = rows - DKV, (owners - 1) * pair_most
    half = rows // 2

    def owner_row(m):
        at = chip ^ m
        return jnp.concatenate(
            [all_ref[at, rows + 1 : rows + 2, :half], all_ref[at, rows + 2 : rows + 3, :half]], axis=1
        )

    lane = iota((rows, rows), 1)
    row = iota((rows, rows), 0)
    earlier = ((row < lane) & (row // block == lane // block)).astype(F32).astype(BF16)
    named = jnp.concatenate(
        [owner_row(m) for m in range(heads)] + [jnp.full((8 - heads, rows), -1.0, F32)], axis=0
    )
    mine = named == z.astype(F32)
    before = jnp.dot(mine.astype(F32).astype(BF16), earlier, preferred_element_type=F32)
    at = iota((8, rows), 1) // block * pair_most
    slot_of = jnp.where(mine, before + at.astype(F32), -1.0)
    slot_id = iota((slots, rows), 0).astype(F32)
    all1 = rows - split + slots - cut
    for m in range(heads):
        terms = all_ref[chip ^ m, :rows, :].astype(BF16)
        pick = (slot_id == slot_of[m : m + 1, :]).astype(F32)
        chosen = jnp.dot(pick.astype(BF16), terms, preferred_element_type=F32).astype(BF16)
        row_ref[m * split : (m + 1) * split, :] = terms[:split]
        slot_ref[m * cut : (m + 1) * cut, :] = chosen[:cut]
        last_ref[m * all1 : m * all1 + rows - split, :] = terms[split:]
        last_ref[m * all1 + rows - split : (m + 1) * all1, :] = chosen[cut:]
        if m == 0:
            live_ref[...] = jnp.sum(pick, axis=1, keepdims=True)
    state = all_ref[chip, rows : rows + 1, :slots]
    same = iota((slots, slots), 0) == iota((slots, slots), 1)
    state_ref[...] = jnp.sum(jnp.where(same, state, 0.0), axis=1, keepdims=True)
    owner_of = jnp.where(
        iota((8, rows), 0) == 0,
        z,
        jnp.where(
            iota((8, rows), 0) == 1,
            (z + owners - 1) % owners,
            jnp.where(iota((8, rows), 0) == 2, (z + 1) % owners, (z + 2) % owners),
        ),
    ).astype(F32)
    theirs = (owner_row(0) == owner_of).astype(F32).astype(BF16)
    home = (iota((rows, slots), 0) // block == iota((rows, slots), 1) // pair_most).astype(F32)
    count = jnp.dot(theirs, home.astype(BF16), preferred_element_type=F32)
    held = (iota((8, slots), 1) % pair_most).astype(F32) < count
    states = [
        all_ref[chip, rows : rows + 1, k * tokens : k * tokens + slots] for k in range(owners)
    ]
    states = jnp.concatenate(states + [jnp.zeros((8 - owners, slots), F32)], axis=0)
    states = jnp.where(held, states, 0.0)
    for i in range(owners):
        part = jnp.where(iota((8, slots), 1) // pair_most == i, states, 0.0)
        part = jnp.sum(jnp.sum(part, axis=1, keepdims=True), axis=0, keepdims=True)
        total_ref[i : i + 1, :] = jnp.broadcast_to(part, (1, slots))


def gather_blocks(held, own, near, got):
    z, _, _ = here_of()
    tokens, half = own.shape
    count = len(got) // 2
    above = jnp.where(z == 3, 1, 2)
    places = (above, 3, 3 - above)
    for side, mine in enumerate((own, near)):
        some = slice(side * half, (side + 1) * half)
        held[:tokens, some] = mine[...].astype(BF16)
        at = 0
        for ref in got[side * count : (side + 1) * count]:
            size = ref.shape[0]
            block, rest = at // tokens, at % tokens
            start = pl.multiple_of(places[block] * tokens + rest, size)
            held[pl.ds(start, size), some] = ref[...].astype(BF16)
            at += size


def multiply(blocks, slot_terms, own, near, *refs):
    got, outs, held = refs[:blocks], refs[blocks:-1], refs[-1]
    gather_blocks(held, own, near, got)
    x = held[...]
    each = outs[0].shape[0]
    g = jnp.dot(slot_terms[...], x, preferred_element_type=F32)
    for m, out in enumerate(outs):
        out[...] = g[m * each : (m + 1) * each]


def column_sums(heads, row_terms, held, sums_ref):
    x = held[...]
    each = row_terms.shape[0] // heads
    every = jnp.dot(row_terms[...], x, preferred_element_type=F32)
    for m in range(heads):
        for p in range(PROJ - 1):
            part = every[m * each + p * DKV : m * each + (p + 1) * DKV]
            sums_ref[m, p : p + 1, :] = jnp.sum(part * part + EPS_SQUARE, axis=0, keepdims=True)


def multiply_last(blocks, slots, terms, own, near, *refs):
    got, sums_ref, outs, held = refs[:blocks], refs[blocks], refs[blocks + 1 : -1], refs[-1]
    gather_blocks(held, own, near, got)
    x = held[...]
    each = DKV + slots
    width = x.shape[1]
    base = width // 128 * slots
    every = jnp.dot(terms[...], x, preferred_element_type=F32)
    for m, out in enumerate(outs):
        g = every[m * each : (m + 1) * each]
        part = g[:DKV]
        last = jnp.sum(part * part + EPS_SQUARE, axis=0, keepdims=True)
        sums = jnp.concatenate([sums_ref[m, : PROJ - 1, :], last], axis=0)
        for j in range(width // 128):
            out[j * slots : (j + 1) * slots, :] = g[DKV:, j * 128 : (j + 1) * 128]
            out[base + j * PROJ : base + (j + 1) * PROJ, :] = sums[:, j * 128 : (j + 1) * 128]


def spans_of(refs, width):
    _, chip, core = here_of()
    heads = len(refs)
    span = width // heads
    half = span // 2
    return [
        (refs[m], side * half, pl.multiple_of((chip ^ m) * span + (core ^ side) * half, 128))
        for m in range(heads)
        for side in range(2)
    ], half


def early(*refs):
    *first, square_ref = refs
    square = jnp.zeros((square_ref.shape[0], 128), F32)
    for ref in first:
        for j in range(0, ref.shape[1], 128):
            g = ref[:, j : j + 128]
            square += g * g + EPS_SQUARE
    square_ref[...] = jnp.sum(square, axis=1, keepdims=True)


def update(heads, pair_most, *refs):
    first, last, refs = refs[:heads], refs[heads : 2 * heads], refs[2 * heads :]
    square0, params, live_ref, state_ref, total_ref, cols, new_params, new_rows, new_cols = refs
    slots, width = params.shape
    rest = pair_most
    span = width // heads
    base = span // 128 * rest
    spans, half = spans_of(first, width)
    spans = [(m, lo, start) for m in range(heads) for _, lo, start in spans[2 * m : 2 * m + 2]]

    def beside(m, lo, offset, count):
        blocks = range(lo // 128, (lo + half) // 128)
        return jnp.concatenate(
            [last[m][offset + j * count : offset + (j + 1) * count, :] for j in blocks], axis=1
        )

    sums = jnp.zeros((PROJ, 128), F32)
    square = jnp.zeros((rest, 128), F32)
    for m, lo, start in spans:
        for j in range(lo // 128, (lo + half) // 128):
            g = last[m][j * rest : (j + 1) * rest, :]
            square += g * g + EPS_SQUARE
            sums += last[m][base + j * PROJ : base + (j + 1) * PROJ, :]
        new_cols[:, pl.ds(start, half)] = (
            DECAY_RATE * cols[:, pl.ds(start, half)]
            + (1.0 - DECAY_RATE) * beside(m, lo, base, PROJ) / DKV
        )
    square = jnp.concatenate([square0[...], jnp.sum(square, axis=1, keepdims=True)], axis=0)
    row_val = DECAY_RATE * state_ref[...] + (1.0 - DECAY_RATE) * (square / width)
    row_mean = (
        DECAY_RATE * total_ref[:, :1]
        + (1.0 - DECAY_RATE) * jnp.sum(sums, axis=1, keepdims=True) / width
    ) / DKV
    mean_at = jnp.concatenate(
        [jnp.broadcast_to(row_mean[i : i + 1], (pair_most, 1)) for i in range(PROJ)], axis=0
    )
    live = live_ref[...]
    row_scale = STEP_SIZE * jnp.sqrt(mean_at / row_val)
    same = iota((slots, slots), 0) == iota((slots, slots), 1)
    new_rows[...] = jnp.sum(jnp.where(same, row_val * live, 0.0), axis=0, keepdims=True)
    for m, lo, start in spans:
        col_scale = lax.rsqrt(new_cols[:, pl.ds(start, half)])
        for i in range(PROJ):
            rows = slice(i * pair_most, (i + 1) * pair_most)
            g = first[m][rows, lo : lo + half] if i < PROJ - 1 else beside(m, lo, 0, rest)
            value = params[rows, pl.ds(start, half)].astype(F32) - g * row_scale[rows] * (
                col_scale[i : i + 1]
            )
            new_params[rows, pl.ds(start, half)] = jnp.where(live[rows] > 0.0, value, 0.0).astype(
                BF16
            )


def gather_step(
    dp_count, shard_count, head_terms, inputs, owner_list, param_slots, row_state, col_state
):
    heads = shard_count // 2
    tokens, _, width = inputs.shape
    rows = head_terms.shape[2]
    slots = param_slots.shape[1]
    pair_most = slots // dp_count
    span = width // heads
    half = span // 2
    split, cut = rows - DKV, slots - pair_most
    depth = dp_count * tokens

    def move(array, dp_to, shard_to=lambda j: j):
        pairs = [
            (i * shard_count + j, dp_to[i] * shard_count + shard_to(j))
            for i in dp_to
            for j in range(shard_count)
        ]
        return lax.ppermute(array, ("dp", "shard"), pairs)

    every = {i: i for i in range(4)}
    upward, downward = {i: i + 1 for i in range(3)}, {i + 1: i for i in range(3)}
    swap = lambda j: j ^ 1

    anywhere = pl.BlockSpec(memory_space=pl.ANY)
    in_vmem = pl.BlockSpec(memory_space=pltpu.VMEM)
    terms = pl.pallas_call(
        functools.partial(begin, rows),
        out_shape=jax.ShapeDtypeStruct((rows + EXTRA, tokens), F32),
        in_specs=[anywhere] * 3,
        out_specs=in_vmem,
        scratch_shapes=[
            pltpu.VMEM((tokens, rows), BF16),
            pltpu.VMEM((1, rows), jnp.int32),
            pltpu.VMEM((1, tokens), F32),
            pltpu.SemaphoreType.DMA((3,)),
        ],
        compiler_params=pltpu.CompilerParams(vmem_limit_bytes=BEGIN_LIMIT),
    )(head_terms[:, 0, :], owner_list[:, :, 0], row_state)
    own0, near0, own1, near1 = pl.pallas_call(
        columns,
        out_shape=[jax.ShapeDtypeStruct((tokens, half), kind) for kind in (F32, BF16)] * 2,
        in_specs=[anywhere],
        out_specs=[in_vmem] * 4,
        scratch_shapes=[pltpu.VMEM((tokens, 2, span), BF16), pltpu.SemaphoreType.DMA(())],
        compiler_params=pltpu.CompilerParams(vmem_limit_bytes=BEGIN_LIMIT),
    )(inputs)

    chips = [[2 * i + c for i in range(heads)] for c in range(2)]
    ring = lambda k: {i: (i + k) % dp_count for i in range(dp_count)}
    def exchange(*blocks):
        size = sum(block.shape[1] for block in blocks)
        everywhere = call(
            spread,
            jax.ShapeDtypeStruct((heads, rows + EXTRA, size), F32),
            arrays=len(blocks),
        )(*blocks)
        return lax.all_to_all(everywhere, "shard", 0, 0, axis_index_groups=chips)

    def chosen(body, parts, cost, *arrays):
        outs = [jax.ShapeDtypeStruct((tokens // parts, half), F32)] * parts
        here = call(body, outs, arrays=len(arrays), flops=cost)(*arrays)
        return here, [move(block, every, swap) for block in here]

    def joined(cost, before, parts, up1, down1, up2, down2, up3, down3):
        one, one_n = chosen(near_one, 1, before, up1, down1)
        two, two_n = chosen(two_away, 1, before, up2, down2)
        three, three_n = chosen(last_one, parts, cost, up1, up3, down3)
        return *one, *two, *three, *one_n, *two_n, *three_n

    def scatter(outs):
        return [
            out if m == 0 else move(out, every, lambda j, m=m: j ^ (2 * m))
            for m, out in enumerate(outs)
        ]

    up1, down1 = move(own0, upward), move(own0, downward)
    ha, hb, hc = [move(terms, ring(k)) for k in (1, dp_count - 1, 2)]
    gathered = exchange(terms, ha, hb, hc)
    up2, down2 = move(up1, upward), move(down1, downward)
    late = lax.optimization_barrier((own1, hc))[0]
    nup1, ndown1 = move(late, upward), move(late, downward)
    up3, down3 = move(up2, upward), move(down2, downward)
    blocks0 = joined(COLLECT_FIRST, NEAR_FIRST, 1, up1, down1, up2, down2, up3, down3)
    nup2, ndown2 = move(nup1, upward), move(ndown1, downward)
    slot_terms, row_terms, last_terms, live, state, total = call(
        functools.partial(prepare, heads, rows, pair_most),
        [
            jax.ShapeDtypeStruct((heads * cut, depth), BF16),
            jax.ShapeDtypeStruct((heads * split, depth), BF16),
            jax.ShapeDtypeStruct((heads * (rows - split + slots - cut), depth), BF16),
            jax.ShapeDtypeStruct((slots, 1), F32),
            jax.ShapeDtypeStruct((slots, 1), F32),
            jax.ShapeDtypeStruct((PROJ, slots), F32),
        ],
        arrays=1,
    )(gathered)
    *outs, held0 = call(
        functools.partial(multiply, len(blocks0)),
        [jax.ShapeDtypeStruct((cut, span), F32)] * heads + [jax.ShapeDtypeStruct((depth, span), BF16)],
        arrays=3 + len(blocks0),
        flops=MULTIPLY_FIRST,
    )(slot_terms, own0, near0, *blocks0)
    sums0 = call(
        functools.partial(column_sums, heads),
        jax.ShapeDtypeStruct((heads, 8, span), F32),
        arrays=2,
    )(row_terms, held0)
    first = scatter(outs)
    nup3, ndown3 = move(nup2, upward), move(ndown2, downward)
    blocks1 = joined(COLLECT_LAST, NEAR_LAST, 2, nup1, ndown1, nup2, ndown2, nup3, ndown3)
    rest = slots - cut
    last = scatter(
        call(
            functools.partial(multiply_last, len(blocks1), rest),
            [jax.ShapeDtypeStruct((span // 128 * (rest + PROJ), 128), F32)] * heads,
            scratch=[pltpu.VMEM((depth, span), BF16)],
            arrays=4 + len(blocks1),
            flops=MULTIPLY_LAST,
        )(last_terms, own1, near1, *blocks1, sums0)
    )
    square0 = call(
        early,
        jax.ShapeDtypeStruct((cut, 1), F32),
        arrays=heads,
    )(*first)
    new_params, new_rows, new_cols = call(
        functools.partial(update, heads, pair_most),
        [
            jax.ShapeDtypeStruct((slots, width), BF16),
            jax.ShapeDtypeStruct((1, slots), F32),
            jax.ShapeDtypeStruct((PROJ, width), F32),
        ],
        arrays=2 * heads + 6,
        moved=4 * slots * width * 2,
    )(*first, *last, square0, param_slots[0], live, state, total, col_state[0])
    return (new_params[None], new_rows, new_cols[None])


def one_step(mesh, *args):
    dp_count, shard_count = mesh.shape["dp"], mesh.shape["shard"]
    tokens, slots, rows = args[1].shape[0], args[3].shape[1], args[0].shape[2]
    if dp_count == 4 and shard_count == 8 and tokens == slots and rows == PROJ * DKV:
        return gather_step(dp_count, shard_count, *args)
    return general_step(*args)


def solution(mesh):
    placed = (
        P("dp", "shard", None),
        P("dp", None, None),
        P("shard", None, None),
        P("shard", "dp", None),
        P("shard", "dp"),
        P("shard", None, None),
    )
    return jax.shard_map(
        functools.partial(one_step, mesh),
        mesh=mesh,
        in_specs=placed,
        out_specs=(P("shard", "dp", None), P("shard", "dp"), P("shard", None, None)),
        check_vma=False,
    )
```

```python
import functools

import jax
import jax.numpy as jnp
from jax import lax
from jax.experimental import pallas as pl
from jax.experimental.pallas import tpu as pltpu
from jax.sharding import PartitionSpec as P

DKV = 64
PROJ = 4


DECAY_RATE = 0.5
STEP_SIZE = 0.5
EPS_SQUARE = 1e-30


def slot_table(owner_col, owner_count, pair_most):
    row_count = owner_col.shape[0]
    block_rows = row_count // owner_count
    index_ids = jnp.arange(owner_count, dtype=jnp.int32)
    onehot = (owner_col[:, None] == index_ids[None, :]).astype(jnp.int32)
    blocked = onehot.reshape(owner_count, block_rows, owner_count)
    before = jnp.cumsum(blocked, axis=1) - blocked
    order_in = jnp.sum(before * blocked, axis=2).reshape(row_count)
    row_ids = jnp.arange(row_count, dtype=jnp.int32)
    block_of = row_ids // block_rows
    slot_ids = jnp.arange(pair_most, dtype=jnp.int32)
    match_owner = owner_col[None, None, None, :] == index_ids[:, None, None, None]
    match_block = block_of[None, None, None, :] == index_ids[None, :, None, None]
    match_slot = order_in[None, None, None, :] == slot_ids[None, None, :, None]
    hits = (match_owner & match_block & match_slot).astype(jnp.int32)
    live_mask = jnp.sum(hits, axis=3).reshape(owner_count, owner_count * pair_most)
    slot_row = jnp.sum(hits * row_ids[None, None, None, :], axis=3).reshape(
        owner_count, owner_count * pair_most
    )
    return (slot_row, live_mask)


def general_step(head_terms, inputs, owner_list, param_slots, row_state, col_state):
    dp_count = lax.axis_size("dp")
    my_index = lax.axis_index("dp")
    head_rows = head_terms[:, 0, :]
    row_count = head_rows.shape[1]
    width = inputs.shape[2]
    slot_count = param_slots.shape[1]
    pair_most = slot_count // dp_count
    block_rows = row_count // dp_count
    split_at = (PROJ - 1) * DKV
    first_part = jnp.einsum(
        "tr,td->rd", head_rows[:, :split_at], inputs[:, 0, :], preferred_element_type=jnp.float32
    )
    last_part = jnp.einsum(
        "tr,td->rd", head_rows[:, split_at:], inputs[:, 1, :], preferred_element_type=jnp.float32
    )
    gradient = jnp.concatenate([first_part, last_part], axis=0)
    slot_row, live_mask = slot_table(owner_list[0, :, 0], dp_count, pair_most)
    home_sum = lax.psum_scatter(gradient, "dp", scatter_dimension=0, tiled=True)
    local_rows = (
        lax.dynamic_slice_in_dim(slot_row, my_index * pair_most, pair_most, 1)
        - my_index * block_rows
    )
    outgoing = jnp.take(home_sum, local_rows.reshape(-1), axis=0, mode="clip").reshape(
        dp_count, pair_most, width
    )
    received = lax.all_to_all(outgoing, "dp", split_axis=0, concat_axis=0, tiled=True)
    slot_grad = received.reshape(slot_count, width)
    my_rows = lax.dynamic_index_in_dim(slot_row, my_index, 0, keepdims=False)
    live_f = lax.dynamic_index_in_dim(live_mask, my_index, 0, keepdims=False).astype(jnp.float32)
    grad_sq = slot_grad * slot_grad + EPS_SQUARE
    row_val = DECAY_RATE * row_state[0] + (1.0 - DECAY_RATE) * jnp.mean(grad_sq, axis=1)
    slot_pick = ((my_rows // DKV)[:, None] == jnp.arange(PROJ, dtype=jnp.int32)[None, :]).astype(
        jnp.float32
    )
    live_pick = slot_pick * live_f[:, None]
    col_part = jnp.einsum("sp,sd->pd", live_pick, grad_sq, precision=lax.Precision.HIGHEST)
    row_part = jnp.sum(live_pick * row_val[:, None], axis=0)
    col_sum, row_total = lax.psum((col_part, row_part), "dp")
    new_col = DECAY_RATE * col_state[0] + (1.0 - DECAY_RATE) * col_sum / DKV
    row_mean = row_total / DKV
    col_at = jnp.dot(slot_pick, new_col, precision=lax.Precision.HIGHEST)
    mean_at = jnp.sum(slot_pick * row_mean[None, :], axis=1)
    second_moment = row_val[:, None] * col_at / mean_at[:, None]
    update = slot_grad / jnp.sqrt(second_moment)
    new_param = (
        (param_slots[0].astype(jnp.float32) - STEP_SIZE * update) * live_f[:, None]
    ).astype(jnp.bfloat16)
    return (new_param[None], (row_val * live_f)[None], new_col[None])


EXTRA = 8
COLLECT_FIRST = 6_400_000_000
COLLECT_LAST = 3_000_000_000
NEAR_FIRST = 1_000_000_000
NEAR_LAST = 0
MULTIPLY_FIRST = 1_300_000_000
MULTIPLY_LAST = 1_000_000_000
BF16 = jnp.bfloat16
F32 = jnp.float32
VMEM_LIMIT = 16 * 1024 * 1024
BEGIN_LIMIT = 56 * 1024 * 1024


def here_of():
    s = lax.axis_index("shard")
    return lax.axis_index("dp"), s // 2, s % 2


def call(body, out_shape, scratch=(), arrays=0, flops=0, moved=0):
    return pl.pallas_call(
        body,
        out_shape=out_shape,
        in_specs=[pl.BlockSpec(memory_space=pltpu.VMEM)] * arrays,
        out_specs=jax.tree.map(lambda _: pl.BlockSpec(memory_space=pltpu.VMEM), out_shape),
        scratch_shapes=list(scratch),
        compiler_params=pltpu.CompilerParams(vmem_limit_bytes=VMEM_LIMIT),
        cost_estimate=pl.CostEstimate(flops=flops, bytes_accessed=moved, transcendentals=0),
    )


def iota(shape, dim):
    return lax.broadcasted_iota(jnp.int32, shape, dim)


def begin(rows, heads_hbm, owner_hbm, state_hbm, terms_ref, heads_ref, owner_ref, state_ref, sems):
    copies = [
        pltpu.make_async_copy(heads_hbm, heads_ref, sems.at[0]),
        pltpu.make_async_copy(owner_hbm, owner_ref, sems.at[1]),
        pltpu.make_async_copy(state_hbm, state_ref, sems.at[2]),
    ]
    for copy in copies:
        copy.start()
    for copy in copies:
        copy.wait()
    terms_ref[:rows, :] = heads_ref[...].astype(F32).T
    terms_ref[rows : rows + 1, :] = state_ref[...]
    named = owner_ref[...].astype(F32)
    terms_ref[rows + 1 : rows + 2, :] = named[:, : rows // 2]
    terms_ref[rows + 2 : rows + 3, :] = named[:, rows // 2 :]
    terms_ref[rows + 3 :, :] = jnp.zeros((terms_ref.shape[0] - rows - 3, terms_ref.shape[1]), F32)


def columns(inputs_hbm, *refs):
    *outs, inputs_ref, sem = refs
    _, chip, core = here_of()
    half = outs[0].shape[1]
    span = 2 * half
    some = pl.ds(pl.multiple_of(chip * span, 128), span)
    copy = pltpu.make_async_copy(inputs_hbm.at[:, :, some], inputs_ref, sem)
    copy.start()
    copy.wait()
    for c in range(2):
        sent, own, near = outs[3 * c : 3 * c + 3]
        at = pl.multiple_of(core * half, 128)
        mine = inputs_ref[:, c, pl.ds(at, half)].astype(F32)
        sent[...] = mine
        own[...] = mine.astype(BF16)
        at = pl.multiple_of((1 - core) * half, 128)
        near[...] = inputs_ref[:, c, pl.ds(at, half)].astype(F32).astype(BF16)


def spread(*refs):
    *blocks, out_ref = refs
    at = 0
    for block in blocks:
        value = block[...]
        for j in range(out_ref.shape[0]):
            out_ref[j, :, at : at + value.shape[1]] = value
        at += value.shape[1]


def near_one(up1, down1, out_ref):
    z, _, _ = here_of()
    out_ref[...] = jnp.where(z <= 2, down1[...], up1[...])


def two_away(up2, down2, out_ref):
    z, _, _ = here_of()
    out_ref[...] = jnp.where(z <= 1, down2[...], up2[...])


def last_one(up1, up3, down3, *outs):
    z, _, _ = here_of()
    value = jnp.where(z == 0, down3[...], jnp.where(z == 3, up3[...], up1[...]))
    size = outs[0].shape[0]
    for i, out in enumerate(outs):
        out[...] = value[i * size : (i + 1) * size]


def prepare(heads, rows, pair_most, all_ref, *refs):
    slot_ref, row_ref, last_ref, live_ref, state_ref, total_ref = refs
    z, chip, _ = here_of()
    owners = rows // DKV
    tokens = all_ref.shape[2] // owners
    block = rows // owners
    slots = owners * pair_most
    split, cut = rows - DKV, (owners - 1) * pair_most
    half = rows // 2

    def owner_row(m):
        at = chip ^ m
        return jnp.concatenate(
            [all_ref[at, rows + 1 : rows + 2, :half], all_ref[at, rows + 2 : rows + 3, :half]], axis=1
        )

    lane = iota((rows, rows), 1)
    row = iota((rows, rows), 0)
    earlier = ((row < lane) & (row // block == lane // block)).astype(F32).astype(BF16)
    named = jnp.concatenate(
        [owner_row(m) for m in range(heads)] + [jnp.full((8 - heads, rows), -1.0, F32)], axis=0
    )
    mine = named == z.astype(F32)
    before = jnp.dot(mine.astype(F32).astype(BF16), earlier, preferred_element_type=F32)
    at = iota((8, rows), 1) // block * pair_most
    slot_of = jnp.where(mine, before + at.astype(F32), -1.0)
    slot_id = iota((slots, rows), 0).astype(F32)
    all1 = rows - split + slots - cut
    for m in range(heads):
        terms = all_ref[chip ^ m, :rows, :].astype(BF16)
        pick = (slot_id == slot_of[m : m + 1, :]).astype(F32)
        chosen = jnp.dot(pick.astype(BF16), terms, preferred_element_type=F32).astype(BF16)
        row_ref[m * split : (m + 1) * split, :] = terms[:split]
        slot_ref[m * cut : (m + 1) * cut, :] = chosen[:cut]
        last_ref[m * all1 : m * all1 + rows - split, :] = terms[split:]
        last_ref[m * all1 + rows - split : (m + 1) * all1, :] = chosen[cut:]
        if m == 0:
            live_ref[...] = jnp.sum(pick, axis=1, keepdims=True)
    state = all_ref[chip, rows : rows + 1, :slots]
    same = iota((slots, slots), 0) == iota((slots, slots), 1)
    state_ref[...] = jnp.sum(jnp.where(same, state, 0.0), axis=1, keepdims=True)
    owner_of = jnp.where(
        iota((8, rows), 0) == 0,
        z,
        jnp.where(
            iota((8, rows), 0) == 1,
            (z + owners - 1) % owners,
            jnp.where(iota((8, rows), 0) == 2, (z + 1) % owners, (z + 2) % owners),
        ),
    ).astype(F32)
    theirs = (owner_row(0) == owner_of).astype(F32).astype(BF16)
    home = (iota((rows, slots), 0) // block == iota((rows, slots), 1) // pair_most).astype(F32)
    count = jnp.dot(theirs, home.astype(BF16), preferred_element_type=F32)
    held = (iota((8, slots), 1) % pair_most).astype(F32) < count
    states = [
        all_ref[chip, rows : rows + 1, k * tokens : k * tokens + slots] for k in range(owners)
    ]
    states = jnp.concatenate(states + [jnp.zeros((8 - owners, slots), F32)], axis=0)
    states = jnp.where(held, states, 0.0)
    for i in range(owners):
        part = jnp.where(iota((8, slots), 1) // pair_most == i, states, 0.0)
        part = jnp.sum(jnp.sum(part, axis=1, keepdims=True), axis=0, keepdims=True)
        total_ref[i : i + 1, :] = jnp.broadcast_to(part, (1, slots))


def gather_blocks(held, own, near, got):
    z, _, _ = here_of()
    tokens, half = own.shape
    count = len(got) // 2
    above = jnp.where(z == 3, 1, 2)
    places = (above, 3, 3 - above)
    for side, mine in enumerate((own, near)):
        some = slice(side * half, (side + 1) * half)
        held[:tokens, some] = mine[...].astype(BF16)
        at = 0
        for ref in got[side * count : (side + 1) * count]:
            size = ref.shape[0]
            block, rest = at // tokens, at % tokens
            start = pl.multiple_of(places[block] * tokens + rest, size)
            held[pl.ds(start, size), some] = ref[...].astype(BF16)
            at += size


def multiply(blocks, slot_terms, own, near, *refs):
    got, outs, held = refs[:blocks], refs[blocks:-1], refs[-1]
    gather_blocks(held, own, near, got)
    x = held[...]
    each = outs[0].shape[0]
    g = jnp.dot(slot_terms[...], x, preferred_element_type=F32)
    for m, out in enumerate(outs):
        out[...] = g[m * each : (m + 1) * each]


def column_sums(heads, row_terms, held, sums_ref):
    x = held[...]
    each = row_terms.shape[0] // heads
    every = jnp.dot(row_terms[...], x, preferred_element_type=F32)
    for m in range(heads):
        for p in range(PROJ - 1):
            part = every[m * each + p * DKV : m * each + (p + 1) * DKV]
            sums_ref[m, p : p + 1, :] = jnp.sum(part * part + EPS_SQUARE, axis=0, keepdims=True)


def multiply_last(blocks, slots, terms, own, near, *refs):
    got, sums_ref, outs, held = refs[:blocks], refs[blocks], refs[blocks + 1 : -1], refs[-1]
    gather_blocks(held, own, near, got)
    x = held[...]
    each = DKV + slots
    width = x.shape[1]
    base = width // 128 * slots
    every = jnp.dot(terms[...], x, preferred_element_type=F32)
    for m, out in enumerate(outs):
        g = every[m * each : (m + 1) * each]
        part = g[:DKV]
        last = jnp.sum(part * part + EPS_SQUARE, axis=0, keepdims=True)
        sums = jnp.concatenate([sums_ref[m, : PROJ - 1, :], last], axis=0)
        for j in range(width // 128):
            out[j * slots : (j + 1) * slots, :] = g[DKV:, j * 128 : (j + 1) * 128]
            out[base + j * PROJ : base + (j + 1) * PROJ, :] = sums[:, j * 128 : (j + 1) * 128]


def spans_of(refs, width):
    _, chip, core = here_of()
    heads = len(refs)
    span = width // heads
    half = span // 2
    return [
        (refs[m], side * half, pl.multiple_of((chip ^ m) * span + (core ^ side) * half, 128))
        for m in range(heads)
        for side in range(2)
    ], half


def early(*refs):
    *first, square_ref = refs
    square = jnp.zeros((square_ref.shape[0], 128), F32)
    for ref in first:
        for j in range(0, ref.shape[1], 128):
            g = ref[:, j : j + 128]
            square += g * g + EPS_SQUARE
    square_ref[...] = jnp.sum(square, axis=1, keepdims=True)


def update(heads, pair_most, *refs):
    first, last, refs = refs[:heads], refs[heads : 2 * heads], refs[2 * heads :]
    square0, params, live_ref, state_ref, total_ref, cols, new_params, new_rows, new_cols = refs
    slots, width = params.shape
    rest = pair_most
    span = width // heads
    base = span // 128 * rest
    spans, half = spans_of(first, width)
    spans = [(m, lo, start) for m in range(heads) for _, lo, start in spans[2 * m : 2 * m + 2]]

    def beside(m, lo, offset, count):
        blocks = range(lo // 128, (lo + half) // 128)
        return jnp.concatenate(
            [last[m][offset + j * count : offset + (j + 1) * count, :] for j in blocks], axis=1
        )

    sums = jnp.zeros((PROJ, 128), F32)
    square = jnp.zeros((rest, 128), F32)
    for m, lo, start in spans:
        for j in range(lo // 128, (lo + half) // 128):
            g = last[m][j * rest : (j + 1) * rest, :]
            square += g * g + EPS_SQUARE
            sums += last[m][base + j * PROJ : base + (j + 1) * PROJ, :]
        new_cols[:, pl.ds(start, half)] = (
            DECAY_RATE * cols[:, pl.ds(start, half)]
            + (1.0 - DECAY_RATE) * beside(m, lo, base, PROJ) / DKV
        )
    square = jnp.concatenate([square0[...], jnp.sum(square, axis=1, keepdims=True)], axis=0)
    row_val = DECAY_RATE * state_ref[...] + (1.0 - DECAY_RATE) * (square / width)
    row_mean = (
        DECAY_RATE * total_ref[:, :1]
        + (1.0 - DECAY_RATE) * jnp.sum(sums, axis=1, keepdims=True) / width
    ) / DKV
    mean_at = jnp.concatenate(
        [jnp.broadcast_to(row_mean[i : i + 1], (pair_most, 1)) for i in range(PROJ)], axis=0
    )
    live = live_ref[...]
    row_scale = STEP_SIZE * jnp.sqrt(mean_at / row_val)
    same = iota((slots, slots), 0) == iota((slots, slots), 1)
    new_rows[...] = jnp.sum(jnp.where(same, row_val * live, 0.0), axis=0, keepdims=True)
    for m, lo, start in spans:
        col_scale = lax.rsqrt(new_cols[:, pl.ds(start, half)])
        for i in range(PROJ):
            rows = slice(i * pair_most, (i + 1) * pair_most)
            g = first[m][rows, lo : lo + half] if i < PROJ - 1 else beside(m, lo, 0, rest)
            value = params[rows, pl.ds(start, half)].astype(F32) - g * row_scale[rows] * (
                col_scale[i : i + 1]
            )
            new_params[rows, pl.ds(start, half)] = jnp.where(live[rows] > 0.0, value, 0.0).astype(
                BF16
            )


def gather_step(
    dp_count, shard_count, head_terms, inputs, owner_list, param_slots, row_state, col_state
):
    heads = shard_count // 2
    tokens, _, width = inputs.shape
    rows = head_terms.shape[2]
    slots = param_slots.shape[1]
    pair_most = slots // dp_count
    span = width // heads
    half = span // 2
    split, cut = rows - DKV, slots - pair_most
    depth = dp_count * tokens

    def move(array, dp_to, shard_to=lambda j: j):
        pairs = [
            (i * shard_count + j, dp_to[i] * shard_count + shard_to(j))
            for i in dp_to
            for j in range(shard_count)
        ]
        return lax.ppermute(array, ("dp", "shard"), pairs)

    every = {i: i for i in range(4)}
    upward, downward = {i: i + 1 for i in range(3)}, {i + 1: i for i in range(3)}
    swap = lambda j: j ^ 1

    anywhere = pl.BlockSpec(memory_space=pl.ANY)
    in_vmem = pl.BlockSpec(memory_space=pltpu.VMEM)
    terms = pl.pallas_call(
        functools.partial(begin, rows),
        out_shape=jax.ShapeDtypeStruct((rows + EXTRA, tokens), F32),
        in_specs=[anywhere] * 3,
        out_specs=in_vmem,
        scratch_shapes=[
            pltpu.VMEM((tokens, rows), BF16),
            pltpu.VMEM((1, rows), jnp.int32),
            pltpu.VMEM((1, tokens), F32),
            pltpu.SemaphoreType.DMA((3,)),
        ],
        compiler_params=pltpu.CompilerParams(vmem_limit_bytes=BEGIN_LIMIT),
    )(head_terms[:, 0, :], owner_list[:, :, 0], row_state)
    sent0, own0, near0, sent1, own1, near1 = pl.pallas_call(
        columns,
        out_shape=[jax.ShapeDtypeStruct((tokens, half), kind) for kind in (F32, BF16, BF16)] * 2,
        in_specs=[anywhere],
        out_specs=[in_vmem] * 6,
        scratch_shapes=[pltpu.VMEM((tokens, 2, span), BF16), pltpu.SemaphoreType.DMA(())],
        compiler_params=pltpu.CompilerParams(vmem_limit_bytes=BEGIN_LIMIT),
    )(inputs)

    chips = [[2 * i + c for i in range(heads)] for c in range(2)]
    ring = lambda k: {i: (i + k) % dp_count for i in range(dp_count)}
    def exchange(*blocks):
        size = sum(block.shape[1] for block in blocks)
        everywhere = call(
            spread,
            jax.ShapeDtypeStruct((heads, rows + EXTRA, size), F32),
            arrays=len(blocks),
        )(*blocks)
        return lax.all_to_all(everywhere, "shard", 0, 0, axis_index_groups=chips)

    def chosen(body, parts, cost, *arrays):
        outs = [jax.ShapeDtypeStruct((tokens // parts, half), F32)] * parts
        here = call(body, outs, arrays=len(arrays), flops=cost)(*arrays)
        return here, [move(block, every, swap) for block in here]

    def joined(cost, before, parts, up1, down1, up2, down2, up3, down3):
        one, one_n = chosen(near_one, 1, before, up1, down1)
        two, two_n = chosen(two_away, 1, before, up2, down2)
        three, three_n = chosen(last_one, parts, cost, up1, up3, down3)
        return *one, *two, *three, *one_n, *two_n, *three_n

    def scatter(outs):
        return [
            out if m == 0 else move(out, every, lambda j, m=m: j ^ (2 * m))
            for m, out in enumerate(outs)
        ]

    up1, down1 = move(sent0, upward), move(sent0, downward)
    ha, hb, hc = [move(terms, ring(k)) for k in (1, dp_count - 1, 2)]
    gathered = exchange(terms, ha, hb, hc)
    up2, down2 = move(up1, upward), move(down1, downward)
    late = lax.optimization_barrier((sent1, hc))[0]
    nup1, ndown1 = move(late, upward), move(late, downward)
    up3, down3 = move(up2, upward), move(down2, downward)
    blocks0 = joined(COLLECT_FIRST, NEAR_FIRST, 1, up1, down1, up2, down2, up3, down3)
    nup2, ndown2 = move(nup1, upward), move(ndown1, downward)
    slot_terms, row_terms, last_terms, live, state, total = call(
        functools.partial(prepare, heads, rows, pair_most),
        [
            jax.ShapeDtypeStruct((heads * cut, depth), BF16),
            jax.ShapeDtypeStruct((heads * split, depth), BF16),
            jax.ShapeDtypeStruct((heads * (rows - split + slots - cut), depth), BF16),
            jax.ShapeDtypeStruct((slots, 1), F32),
            jax.ShapeDtypeStruct((slots, 1), F32),
            jax.ShapeDtypeStruct((PROJ, slots), F32),
        ],
        arrays=1,
    )(gathered)
    *outs, held0 = call(
        functools.partial(multiply, len(blocks0)),
        [jax.ShapeDtypeStruct((cut, span), F32)] * heads + [jax.ShapeDtypeStruct((depth, span), BF16)],
        arrays=3 + len(blocks0),
        flops=MULTIPLY_FIRST,
    )(slot_terms, own0, near0, *blocks0)
    sums0 = call(
        functools.partial(column_sums, heads),
        jax.ShapeDtypeStruct((heads, 8, span), F32),
        arrays=2,
    )(row_terms, held0)
    first = scatter(outs)
    nup3, ndown3 = move(nup2, upward), move(ndown2, downward)
    blocks1 = joined(COLLECT_LAST, NEAR_LAST, 2, nup1, ndown1, nup2, ndown2, nup3, ndown3)
    rest = slots - cut
    last = scatter(
        call(
            functools.partial(multiply_last, len(blocks1), rest),
            [jax.ShapeDtypeStruct((span // 128 * (rest + PROJ), 128), F32)] * heads,
            scratch=[pltpu.VMEM((depth, span), BF16)],
            arrays=4 + len(blocks1),
            flops=MULTIPLY_LAST,
        )(last_terms, own1, near1, *blocks1, sums0)
    )
    square0 = call(
        early,
        jax.ShapeDtypeStruct((cut, 1), F32),
        arrays=heads,
    )(*first)
    new_params, new_rows, new_cols = call(
        functools.partial(update, heads, pair_most),
        [
            jax.ShapeDtypeStruct((slots, width), BF16),
            jax.ShapeDtypeStruct((1, slots), F32),
            jax.ShapeDtypeStruct((PROJ, width), F32),
        ],
        arrays=2 * heads + 6,
        moved=4 * slots * width * 2,
    )(*first, *last, square0, param_slots[0], live, state, total, col_state[0])
    return (new_params[None], new_rows, new_cols[None])


def one_step(mesh, *args):
    dp_count, shard_count = mesh.shape["dp"], mesh.shape["shard"]
    tokens, slots, rows = args[1].shape[0], args[3].shape[1], args[0].shape[2]
    if dp_count == 4 and shard_count == 8 and tokens == slots and rows == PROJ * DKV:
        return gather_step(dp_count, shard_count, *args)
    return general_step(*args)


def solution(mesh):
    placed = (
        P("dp", "shard", None),
        P("dp", None, None),
        P("shard", None, None),
        P("shard", "dp", None),
        P("shard", "dp"),
        P("shard", None, None),
    )
    return jax.shard_map(
        functools.partial(one_step, mesh),
        mesh=mesh,
        in_specs=placed,
        out_specs=(P("shard", "dp", None), P("shard", "dp"), P("shard", None, None)),
        check_vma=False,
    )
```
